32 devices in a mesh: blk: 4 (over y, x), grp: 8 (over z, core).
Axes of the slice: x: 2, y: 2, z: 4, core: 2. Of those that a mesh axis runs over, the one named last changes fastest.
Arguments:
- picture_vectors_prenorm: float32 [512, 1152], P(('blk', 'grp')), may hold values from -2 to 2, as said below
- caption_vectors_prenorm: float32 [512, 1152], P(('blk', 'grp')), may hold values from -2 to 2, as said below
- matched_caption_ids: int32 [512], P(('blk', 'grp')), may hold values from 0 to 511, each once
- sharpness_coefficient: float32 [1], replicated, may hold values from 4 to 12
- additive_offset_term: float32 [1], replicated, may hold values from -6 to -2
- heads_mixed_concluding: bfloat16 [12288, 1536], P(('blk', 'grp')), may hold values from -6 to 6
- dense_result_adjoint: bfloat16 [12288, 1536], P(('blk', 'grp')), may hold values from -6 to 6
- dense_mapping_matrix: bfloat16 [1536, 1536], P('grp'), may hold values from -0.15625 to 0.15625
Outputs:
- image_grad: float32 [512, 1152], P(('blk', 'grp'))
- text_grad: float32 [512, 1152], P(('blk', 'grp'))
- attn_grad: bfloat16 [12288, 1536], P(('blk', 'grp'))
- weight_grad: float32 [1536, 1536], P('grp')
The draws below stay inside these ranges and needn't reach their ends.
Inputs may be any that keep to these rules, and one draw needn't show every extreme that they name: `matched_caption_ids`: each text index appears once. `picture_vectors_prenorm`: raw embedding entries. `caption_vectors_prenorm`: raw embedding entries.
All inputs are finite; a program needn't handle non-finite values.
Results may differ from the reference program's by a relative error of at most 0.0053.
Values may be sent and summed in bfloat16 or wider, within the bound.
A program may use at most 128 MiB of HBM per device.

```python
import math
import jax
import jax.numpy as jnp
from jax import lax

EMB = 1152
D = 1536
TOK_DEV = 384
PAIRS = 512
TOKENS = 12288
DEVICES = 32


def draw_picture_vectors_prenorm(key, part):
    key = jax.random.fold_in(key, 17)
    scale_key, entry_key = jax.random.split(key)
    scales = jnp.exp(jax.random.uniform(scale_key, (PAIRS, 1), jnp.float32, math.log(0.3), math.log(3.0)))
    entries = jnp.clip(jax.random.normal(entry_key, (PAIRS, EMB), jnp.float32), -5.0, 5.0)
    return entries * scales / math.sqrt(EMB)


def draw_caption_vectors_prenorm(key, part):
    key = jax.random.fold_in(key, 29)
    scale_key, entry_key = jax.random.split(key)
    scales = jnp.exp(jax.random.uniform(scale_key, (PAIRS, 1), jnp.float32, math.log(0.3), math.log(3.0)))
    entries = jnp.clip(jax.random.normal(entry_key, (PAIRS, EMB), jnp.float32), -5.0, 5.0)
    return entries * scales / math.sqrt(EMB)


def shard_levels(key, shape, pieces, low, top_value):
    def one(dim, blocks):
        heights = jax.random.uniform(jax.random.fold_in(jax.random.fold_in(key, 6), dim), (blocks,), jnp.float32, low / len(pieces), top_value / len(pieces))
        return jnp.repeat(jnp.exp(heights), shape[dim] // blocks).reshape((-1,) + (1,) * (len(shape) - dim - 1))

    level = one(*pieces[0])
    for cut in pieces[1:]:
        level = level * one(*cut)
    return level


def bell_draw(own_key, shape, scale, limit, pieces=(), dtype=jnp.bfloat16):
    factor_of = shard_levels(own_key, shape, pieces, -0.22, 0.18) if pieces else 1.0
    values = jax.random.normal(own_key, shape, jnp.float32) * scale * factor_of
    return jnp.minimum(jnp.maximum(values, -limit), limit).astype(dtype)


def setup_inputs(seed: int = 0) -> dict:
    splits = jax.random.split(jax.random.key(seed), 9)
    picture_vectors_prenorm = draw_picture_vectors_prenorm(jax.random.fold_in(splits[8], 71), 0)
    caption_vectors_prenorm = draw_caption_vectors_prenorm(jax.random.fold_in(splits[8], 71), 0)
    matched_caption_ids = jax.random.permutation(splits[2], PAIRS).astype(jnp.int32)
    sharpness_coefficient = jnp.clip(jax.random.uniform(splits[3], (1,), jnp.float32, 4.0, 12.0), 4.0, 12.0)
    additive_offset_term = jnp.clip(jax.random.uniform(splits[4], (1,), jnp.float32, -6.0, -2.0), -6.0, -2.0)
    heads_mixed_concluding = bell_draw(splits[5], (TOKENS, D), 1.0, 6.0, ((0, 32),))
    dense_result_adjoint = bell_draw(splits[6], (TOKENS, D), 1.0, 6.0, ((0, 32),))
    dense_mapping_matrix = bell_draw(splits[7], (D, D), D ** -0.5, 0.15625, ((0, 8),))
    return dict(picture_vectors_prenorm=picture_vectors_prenorm, caption_vectors_prenorm=caption_vectors_prenorm, matched_caption_ids=matched_caption_ids, sharpness_coefficient=sharpness_coefficient, additive_offset_term=additive_offset_term, heads_mixed_concluding=heads_mixed_concluding, dense_result_adjoint=dense_result_adjoint, dense_mapping_matrix=dense_mapping_matrix)


stability_floor = 1e-06

def unit_rows(raw):
    row_scale = lax.rsqrt(lax.optimization_barrier(jnp.sum(raw * raw, axis=1, keepdims=True)) + stability_floor)
    return (raw * row_scale, row_scale)

def back_through_norm(normed, row_scale, row_grad):
    along_unit = lax.optimization_barrier(jnp.sum(normed * row_grad, axis=1, keepdims=True))
    return (row_grad - normed * along_unit) * row_scale

def weighted_sum(query_half, key_half, labels, sigmoid_multiplier, bias_value):
    inner_dots = lax.dot_general(query_half, key_half, (((1,), (1,)), ((), ())), preferred_element_type=jnp.float32)
    logits = sigmoid_multiplier * inner_dots + bias_value
    pair_weights = (sigmoid_multiplier * (jax.nn.sigmoid(logits) - labels)).astype(jnp.bfloat16)
    return jnp.dot(pair_weights, key_half, preferred_element_type=jnp.float32)

def reference(picture_vectors_prenorm, caption_vectors_prenorm, matched_caption_ids, sharpness_coefficient, additive_offset_term, heads_mixed_concluding, dense_result_adjoint, dense_mapping_matrix):
    image_units, image_scale = unit_rows(picture_vectors_prenorm)
    text_units, text_scale = unit_rows(caption_vectors_prenorm)
    image_half = image_units.astype(jnp.bfloat16)
    text_half = text_units.astype(jnp.bfloat16)
    sigmoid_multiplier = sharpness_coefficient[0]
    bias_value = additive_offset_term[0]
    columns = lax.broadcasted_iota(jnp.int32, (1, PAIRS), 1)
    labels = (matched_caption_ids.astype(jnp.int32)[:, None] == columns).astype(jnp.float32)
    image_unit_grad = weighted_sum(image_half, text_half, labels, sigmoid_multiplier, bias_value)
    text_unit_grad = weighted_sum(text_half, image_half, labels.T, sigmoid_multiplier, bias_value)
    image_grad = back_through_norm(image_units, image_scale, image_unit_grad)
    text_grad = back_through_norm(text_units, text_scale, text_unit_grad)
    attn_grad = lax.dot_general(dense_result_adjoint, dense_mapping_matrix, (((1,), (1,)), ((), ())), preferred_element_type=jnp.float32).astype(jnp.bfloat16)
    attention_block_list = heads_mixed_concluding.reshape(DEVICES, TOK_DEV, D)
    grad_blocks = dense_result_adjoint.reshape(DEVICES, TOK_DEV, D)

    def add_device(total, blocks):
        term = lax.dot_general(blocks[0], blocks[1], (((0,), (0,)), ((), ())), preferred_element_type=jnp.float32)
        return (total + term, None)
    weight_sum, unused = lax.scan(add_device, jnp.zeros((D, D), jnp.float32), (attention_block_list, grad_blocks))
    weight_grad = weight_sum * (1.0 / math.sqrt(TOKENS))
    return (image_grad, text_grad, attn_grad, weight_grad)
```

```python
import functools
import math

import jax
import jax.numpy as jnp
from jax import lax
from jax.experimental import pallas as pl
from jax.experimental.pallas import tpu as pltpu
from jax.sharding import PartitionSpec as P

stability_floor = 1e-06


def as_sent(x):

    def short(part):
        return part.astype(jnp.bfloat16) if part.dtype == jnp.float32 else part

    return jax.tree.map(short, x)


def passed_along(x, axis, by):
    peers = lax.axis_size(axis)
    return lax.ppermute(x, axis, [(i, (i + by) % peers) for i in range(peers)])


def unit_rows(raw):
    row_scale = lax.rsqrt(jnp.sum(raw * raw, axis=1, keepdims=True) + stability_floor)
    return (raw * row_scale, row_scale)


def back_through_norm(normed, row_scale, row_grad):
    along_unit = jnp.sum(normed * row_grad, axis=1, keepdims=True)
    return (row_grad - normed * along_unit) * row_scale


def weighted_sum(query_half, key_half, labels, sigmoid_multiplier, bias_value):
    inner_dots = lax.dot_general(
        query_half, key_half, (((1,), (1,)), ((), ())), preferred_element_type=jnp.float32
    )
    logits = sigmoid_multiplier * inner_dots + bias_value
    pair_weights = (sigmoid_multiplier * (jax.nn.sigmoid(logits) - labels)).astype(jnp.bfloat16)
    return jnp.dot(pair_weights, key_half, preferred_element_type=jnp.float32)


def pass_on(held_rows, direction):
    return jax.tree.map(
        lambda part, own: part.astype(own.dtype),
        passed_along(as_sent(held_rows), "blk", direction),
        held_rows,
    )


def plain_device(
    picture_vectors_prenorm,
    caption_vectors_prenorm,
    matched_caption_ids,
    sharpness_coefficient,
    additive_offset_term,
    heads_mixed_concluding,
    dense_result_adjoint,
    dense_mapping_matrix,
):
    image_units, image_scale = unit_rows(picture_vectors_prenorm)
    text_units, text_scale = unit_rows(caption_vectors_prenorm)
    image_half = image_units.astype(jnp.bfloat16)
    text_half = text_units.astype(jnp.bfloat16)
    sigmoid_multiplier = sharpness_coefficient[0]
    bias_value = additive_offset_term[0]
    own_rows = image_half.shape[0]
    own_first = (lax.axis_index("blk") * lax.axis_size("grp") + lax.axis_index("grp")) * own_rows
    text_index = own_first + lax.broadcasted_iota(jnp.int32, (own_rows, 1), 0)
    grads = (jnp.zeros(image_units.shape, jnp.float32), jnp.zeros(text_units.shape, jnp.float32))
    image_block, text_block, owner_ids = (
        lax.all_gather(image_half, "grp", axis=0, tiled=True),
        lax.all_gather(text_half, "grp", axis=0, tiled=True),
        lax.all_gather(matched_caption_ids, "grp", axis=0, tiled=True),
    )
    group_rows = image_block.shape[0]
    cycle_size = lax.axis_size("blk")
    cycle_place = lax.axis_index("blk")
    streams = [(1, 0, (image_block, text_block, owner_ids))]
    for cycle_step in range(cycle_size):
        next_streams = []
        for direction, offset, held_rows in streams:
            anchor = jnp.remainder(cycle_place - direction * cycle_step, cycle_size)
            absorb_text_block = held_rows[1]
            columns = (
                anchor * group_rows
                + offset
                + lax.broadcasted_iota(jnp.int32, (1, absorb_text_block.shape[0]), 1)
            )
            image_labels = (matched_caption_ids[:, None] == columns).astype(jnp.float32)
            text_labels = (text_index == held_rows[2][None, :]).astype(jnp.float32)
            image_part = weighted_sum(
                image_half, absorb_text_block, image_labels, sigmoid_multiplier, bias_value
            )
            text_part = weighted_sum(
                text_half, held_rows[0], text_labels, sigmoid_multiplier, bias_value
            )
            grads = (grads[0] + image_part, grads[1] + text_part)
            if cycle_step + 1 < cycle_size:
                held_rows = pass_on(held_rows, direction)
            next_streams.append((direction, offset, held_rows))
        streams = next_streams
    image_grad = back_through_norm(image_units, image_scale, grads[0])
    text_grad = back_through_norm(text_units, text_scale, grads[1])
    attn_grad = lax.dot_general(
        dense_result_adjoint,
        lax.all_gather(dense_mapping_matrix, "grp", axis=0, tiled=True),
        (((1,), (1,)), ((), ())),
        preferred_element_type=jnp.float32,
    ).astype(jnp.bfloat16)
    weight_share = lax.psum_scatter(
        lax.dot_general(
            heads_mixed_concluding,
            dense_result_adjoint,
            (((0,), (0,)), ((), ())),
            preferred_element_type=jnp.float32,
        ),
        "grp",
        scatter_dimension=0,
        tiled=True,
    )
    weight_total = lax.psum(weight_share, "blk")
    token_count = heads_mixed_concluding.shape[0] * lax.axis_size("blk") * lax.axis_size("grp")
    weight_grad = weight_total * (1.0 / math.sqrt(token_count))
    return (image_grad, text_grad, attn_grad, weight_grad)


MESH = pl.DeviceIdType.MESH
f32 = jnp.float32
bf16 = jnp.bfloat16


def fused_kernel(
    blks,
    zs,
    scale,
    sharp_ref,
    bias_ref,
    pic_ref,
    cap_ref,
    ids_ref,
    heads_ref,
    adj_ref,
    w_ref,
    pic_out,
    cap_out,
    attn_out,
    wgrad_out,
    heads_t,
    heads_peer,
    adj_peer,
    w_full,
    part,
    part_in,
    zsum,
    zsum_in,
    done,
    emb,
    emb_ids,
    query,
    query_ids,
    pair_grad,
    pair_grad_in,
    core_sem,
    wz_sem,
    wb_sem,
    wc_sem,
    part_sem,
    zsum_sem,
    done_sem,
    ez_sem,
    eb_sem,
):
    b = lax.axis_index("blk")
    g = lax.axis_index("grp")
    z = g // 2
    c = g % 2
    rows = w_ref.shape[0]
    chunk = rows // blks
    wide = 2 * rows
    own = pic_ref.shape[0]

    def blk_peer(d):
        return (lax.rem(b + d, blks), g)

    def z_peer(d):
        return (b, lax.rem(z + d, zs) * 2 + c)

    partner = (b, z * 2 + 1 - c)

    def rcopy(src, dst, sems, to):
        return pltpu.make_async_remote_copy(
            src_ref=src, dst_ref=dst, send_sem=sems.at[0], recv_sem=sems.at[1],
            device_id=to, device_id_type=MESH,
        )

    barrier = pltpu.get_barrier_semaphore()
    peers = [blk_peer(d) for d in range(1, blks)] + [z_peer(d) for d in range(1, zs)] + [partner]
    for peer in peers:
        pl.semaphore_signal(barrier, inc=1, device_id=peer, device_id_type=MESH)

    image_units, image_scale = unit_rows(pic_ref[...])
    text_units, text_scale = unit_rows(cap_ref[...])
    emb[b, z, 0] = image_units.astype(bf16)
    emb[b, z, 1] = text_units.astype(bf16)
    emb_ids[b, z] = ids_ref[...]
    query[c, 0] = image_units.astype(bf16)
    query[c, 1] = text_units.astype(bf16)
    query_ids[c] = ids_ref[...]
    w_full[z, c] = w_ref[...]
    for t in range(zs):
        turned = heads_ref[:, t * wide:(t + 1) * wide].T
        heads_t[0, t] = turned[:rows]
        heads_t[1, t] = turned[rows:]

    pl.semaphore_wait(barrier, len(peers))

    sent = []

    def go(copy):
        copy.start()
        sent.append(copy)
        return copy

    swap_adj = go(rcopy(adj_ref, adj_peer, core_sem.at[0], partner))
    swap_heads = go(rcopy(heads_t.at[1 - c], heads_peer, core_sem.at[1], partner))
    swap_query = go(rcopy(emb.at[b, z], query.at[c], core_sem.at[2], partner))
    swap_ids = go(rcopy(ids_ref, query_ids.at[c], core_sem.at[3], partner))
    for d in range(1, zs):
        go(rcopy(emb.at[b, z], emb.at[b, z], ez_sem.at[d - 1, 0], z_peer(d)))
        go(rcopy(ids_ref, emb_ids.at[b, z], ez_sem.at[d - 1, 1], z_peer(d)))
    mine = pl.ds(pl.multiple_of(b * chunk, 16), chunk)
    for d in range(1, zs):
        go(rcopy(w_ref.at[mine], w_full.at[z, c, mine], wz_sem.at[d - 1], z_peer(d)))
    go(rcopy(w_ref, w_full.at[z, c], wc_sem.at[0], partner))

    swap_adj.wait_recv()
    swap_heads.wait_recv()

    def part_copy(k, d):
        to = blk_peer(d)
        there = pl.ds(pl.multiple_of(to[0] * chunk, 16), chunk)
        return rcopy(part.at[k, there], part_in.at[k, d - 1], part_sem.at[k, d - 1], to)

    cols = adj_ref.shape[1]
    tile = cols // 3 if cols % 384 == 0 else cols

    @pl.loop(0, zs)
    def _(k):
        t = lax.rem(z + 1 + k, zs)
        for j in range(0, cols, tile):
            part[k, :, j:j + tile] = (
                jnp.dot(heads_t[c, t], adj_ref[:, j:j + tile], preferred_element_type=f32)
                + jnp.dot(heads_peer[t], adj_peer[:, j:j + tile], preferred_element_type=f32)
            ).astype(bf16)
        for d in range(1, blks):
            part_copy(k, d).start()

    for d in range(1, zs):
        zf = lax.rem(z + zs - d, zs)
        rcopy(emb.at[b, zf], emb.at[b, zf], ez_sem.at[d - 1, 0], partner).wait_recv()
        rcopy(emb_ids.at[b, zf], emb_ids.at[b, zf], ez_sem.at[d - 1, 1], partner).wait_recv()
    for d in range(1, blks):
        go(rcopy(emb.at[b], emb.at[b], eb_sem.at[d - 1, 0], blk_peer(d)))
        go(rcopy(emb_ids.at[b], emb_ids.at[b], eb_sem.at[d - 1, 1], blk_peer(d)))
    for e in range(1, zs):
        zf = lax.rem(z + zs - e, zs)
        here = w_full.at[zf, c, mine]
        rcopy(here, here, wz_sem.at[e - 1], partner).wait_recv()
        for d in range(1, blks):
            go(rcopy(here, here, wb_sem.at[e - 1, d - 1], blk_peer(d)))

    def own_attn(zf):
        both = w_full[zf].reshape(wide, cols)
        attn_out[:, pl.ds(pl.multiple_of(zf * wide, 128), wide)] = lax.dot_general(
            adj_ref[...], both, (((1,), (1,)), ((), ())), preferred_element_type=f32
        ).astype(bf16)

    rcopy(w_full.at[z, 1 - c], w_full.at[z, 1 - c], wc_sem.at[0], partner).wait_recv()
    own_attn(z)

    for k in range(zs):
        total = part[k, mine].astype(f32)
        for d in range(1, blks):
            part_copy(k, d).wait_recv()
            total += part_in[k, d - 1].astype(f32)
        if k < zs - 1:
            zsum[k] = total.astype(bf16)
            go(rcopy(zsum.at[k], zsum_in.at[k], zsum_sem.at[k], z_peer(k + 1)))

    swap_query.wait_recv()
    swap_ids.wait_recv()
    for d in range(1, blks):
        bf = lax.rem(b + blks - d, blks)
        rcopy(emb.at[bf], emb.at[bf], eb_sem.at[d - 1, 0], partner).wait_recv()
        rcopy(emb_ids.at[bf], emb_ids.at[bf], eb_sem.at[d - 1, 1], partner).wait_recv()
    keys = blks * zs * own
    width = emb.shape[-1]
    image_keys = emb[:, :, 0].reshape(keys, width)
    text_keys = emb[:, :, 1].reshape(keys, width)
    key_ids = emb_ids[...].reshape(keys, ids_ref.shape[1])
    image_query = query[:, 0].reshape(2 * own, width)
    text_query = query[:, 1].reshape(2 * own, width)
    lane = lax.broadcasted_iota(jnp.int32, (2 * own, keys), 1)
    column = (lane // own) * (2 * own) + c * own + lane % own
    image_labels = (query_ids[...].reshape(2 * own, ids_ref.shape[1])[:, :1] == column).astype(f32)
    chip_first = (b * zs + z) * 2 * own
    text_place = chip_first + lax.broadcasted_iota(jnp.int32, key_ids.shape, 1)
    text_labels = (key_ids == text_place).astype(f32).T[: 2 * own]
    sharp = sharp_ref[0]
    bias = bias_ref[0]
    image_part = weighted_sum(image_query, text_keys, image_labels, sharp, bias)
    text_part = weighted_sum(text_query, image_keys, text_labels, sharp, bias)
    pair_grad[:, 0] = image_part.reshape(2, own, width)
    pair_grad[:, 1] = text_part.reshape(2, own, width)
    swap_grad = go(rcopy(pair_grad.at[1 - c], pair_grad_in, core_sem.at[4], partner))

    for e in range(1, zs):
        zf = lax.rem(z + zs - e, zs)
        for d in range(1, blks):
            bf = lax.rem(b + blks - d, blks)
            there = w_full.at[zf, c, pl.ds(pl.multiple_of(bf * chunk, 16), chunk)]
            rcopy(there, there, wb_sem.at[e - 1, d - 1], partner).wait_recv()
        go(rcopy(w_full.at[zf, c], w_full.at[zf, c], wc_sem.at[e], partner))

    for k in range(zs - 1):
        rcopy(zsum.at[k], zsum_in.at[k], zsum_sem.at[k], partner).wait_recv()
        total += zsum_in[k].astype(f32)
    done[0] = (total * scale).astype(bf16)
    for d in range(1, blks):
        go(rcopy(done.at[0], done.at[d], done_sem.at[d - 1], blk_peer(d)))

    for e in range(1, zs):
        zf = lax.rem(z + zs - e, zs)
        there = w_full.at[zf, 1 - c]
        rcopy(there, there, wc_sem.at[e], partner).wait_recv()
        own_attn(zf)

    swap_grad.wait_recv()
    pic_out[...] = back_through_norm(image_units, image_scale, pair_grad[c, 0] + pair_grad_in[0])
    cap_out[...] = back_through_norm(text_units, text_scale, pair_grad[c, 1] + pair_grad_in[1])

    wgrad_out[mine] = done[0].astype(f32)
    for d in range(1, blks):
        bf = lax.rem(b + blks - d, blks)
        rcopy(done.at[0], done.at[d], done_sem.at[d - 1], partner).wait_recv()
        wgrad_out[pl.ds(pl.multiple_of(bf * chunk, 16), chunk)] = done[d].astype(f32)

    for copy in sent:
        copy.wait_send()

    @pl.loop(0, zs)
    def _(k):
        for d in range(1, blks):
            part_copy(k, d).wait_send()


def fused_device(blks, grps, pic, cap, ids, sharp, bias, heads, adj, w):
    zs = grps // 2
    own, width = pic.shape
    tokens, cols = adj.shape
    rows = w.shape[0]
    chunk = rows // blks
    scale = 1.0 / math.sqrt(tokens * blks * grps)
    vmem = pl.BlockSpec(memory_space=pltpu.VMEM)
    smem = pl.BlockSpec(memory_space=pltpu.SMEM)
    dma = pltpu.SemaphoreType.DMA
    flops = 2 * tokens * cols * cols * 2
    return pl.pallas_call(
        functools.partial(fused_kernel, blks, zs, scale),
        out_shape=(
            jax.ShapeDtypeStruct(pic.shape, f32),
            jax.ShapeDtypeStruct(cap.shape, f32),
            jax.ShapeDtypeStruct(heads.shape, bf16),
            jax.ShapeDtypeStruct(w.shape, f32),
        ),
        in_specs=[smem, smem] + [vmem] * 6,
        out_specs=(vmem,) * 4,
        scratch_shapes=[
            pltpu.VMEM((2, zs, rows, tokens), bf16),
            pltpu.VMEM((zs, rows, tokens), bf16),
            pltpu.VMEM((tokens, cols), bf16),
            pltpu.VMEM((zs, 2, rows, cols), bf16),
            pltpu.VMEM((zs, rows, cols), bf16),
            pltpu.VMEM((zs, blks - 1, chunk, cols), bf16),
            pltpu.VMEM((zs - 1, chunk, cols), bf16),
            pltpu.VMEM((zs - 1, chunk, cols), bf16),
            pltpu.VMEM((blks, chunk, cols), bf16),
            pltpu.VMEM((blks, zs, 2, own, width), bf16),
            pltpu.VMEM((blks, zs, own, 128), jnp.int32),
            pltpu.VMEM((2, 2, own, width), bf16),
            pltpu.VMEM((2, own, 128), jnp.int32),
            pltpu.VMEM((2, 2, own, width), f32),
            pltpu.VMEM((2, own, width), f32),
            dma((5, 2)),
            dma((zs - 1, 2)),
            dma((zs - 1, blks - 1, 2)),
            dma((zs, 2)),
            dma((zs, blks - 1, 2)),
            dma((zs - 1, 2)),
            dma((blks - 1, 2)),
            dma((zs - 1, 2, 2)),
            dma((blks - 1, 2, 2)),
        ],
        compiler_params=pltpu.CompilerParams(
            collective_id=0, has_side_effects=True, vmem_limit_bytes=48 * 1024 * 1024
        ),
        cost_estimate=pl.CostEstimate(
            flops=flops, bytes_accessed=8 * tokens * cols, transcendentals=0
        ),
    )(sharp, bias, pic, cap, jnp.broadcast_to(ids[:, None], (own, 128)), heads, adj, w)


def per_device(pic, cap, ids, sharp, bias, heads, adj, w):
    blks = lax.axis_size("blk")
    grps = lax.axis_size("grp")
    own = pic.shape[0]
    rows, cols = w.shape
    fits = (
        grps % 2 == 0
        and grps >= 4
        and blks >= 2
        and rows % (16 * blks) == 0
        and (2 * rows) % 128 == 0
        and heads.shape[1] == rows * grps
        and cols == heads.shape[1]
        and own % 16 == 0
        and 2 * own <= 128
    )
    if not fits:
        return plain_device(pic, cap, ids, sharp, bias, heads, adj, w)
    return fused_device(blks, grps, pic, cap, ids, sharp, bias, heads, adj, w)


def solution(mesh):
    placed = (
        P(("blk", "grp"), None),
        P(("blk", "grp"), None),
        P(("blk", "grp")),
        P(),
        P(),
        P(("blk", "grp"), None),
        P(("blk", "grp"), None),
        P("grp", None),
    )
    return jax.shard_map(
        per_device,
        mesh=mesh,
        in_specs=placed,
        out_specs=(
            P(("blk", "grp"), None),
            P(("blk", "grp"), None),
            P(("blk", "grp"), None),
            P("grp", None),
        ),
        check_vma=False,
    )
```

```python
import functools
import math

import jax
import jax.numpy as jnp
from jax import lax
from jax.experimental import pallas as pl
from jax.experimental.pallas import tpu as pltpu
from jax.sharding import PartitionSpec as P

stability_floor = 1e-06


def as_sent(x):

    def short(part):
        return part.astype(jnp.bfloat16) if part.dtype == jnp.float32 else part

    return jax.tree.map(short, x)


def passed_along(x, axis, by):
    peers = lax.axis_size(axis)
    return lax.ppermute(x, axis, [(i, (i + by) % peers) for i in range(peers)])


def unit_rows(raw):
    row_scale = lax.rsqrt(jnp.sum(raw * raw, axis=1, keepdims=True) + stability_floor)
    return (raw * row_scale, row_scale)


def back_through_norm(normed, row_scale, row_grad):
    along_unit = jnp.sum(normed * row_grad, axis=1, keepdims=True)
    return (row_grad - normed * along_unit) * row_scale


def weighted_sum(query_half, key_half, labels, sigmoid_multiplier, bias_value):
    inner_dots = lax.dot_general(
        query_half, key_half, (((1,), (1,)), ((), ())), preferred_element_type=jnp.float32
    )
    logits = sigmoid_multiplier * inner_dots + bias_value
    pair_weights = (sigmoid_multiplier * (jax.nn.sigmoid(logits) - labels)).astype(jnp.bfloat16)
    return jnp.dot(pair_weights, key_half, preferred_element_type=jnp.float32)


def pass_on(held_rows, direction):
    return jax.tree.map(
        lambda part, own: part.astype(own.dtype),
        passed_along(as_sent(held_rows), "blk", direction),
        held_rows,
    )


def plain_device(
    picture_vectors_prenorm,
    caption_vectors_prenorm,
    matched_caption_ids,
    sharpness_coefficient,
    additive_offset_term,
    heads_mixed_concluding,
    dense_result_adjoint,
    dense_mapping_matrix,
):
    image_units, image_scale = unit_rows(picture_vectors_prenorm)
    text_units, text_scale = unit_rows(caption_vectors_prenorm)
    image_half = image_units.astype(jnp.bfloat16)
    text_half = text_units.astype(jnp.bfloat16)
    sigmoid_multiplier = sharpness_coefficient[0]
    bias_value = additive_offset_term[0]
    own_rows = image_half.shape[0]
    own_first = (lax.axis_index("blk") * lax.axis_size("grp") + lax.axis_index("grp")) * own_rows
    text_index = own_first + lax.broadcasted_iota(jnp.int32, (own_rows, 1), 0)
    grads = (jnp.zeros(image_units.shape, jnp.float32), jnp.zeros(text_units.shape, jnp.float32))
    image_block, text_block, owner_ids = (
        lax.all_gather(image_half, "grp", axis=0, tiled=True),
        lax.all_gather(text_half, "grp", axis=0, tiled=True),
        lax.all_gather(matched_caption_ids, "grp", axis=0, tiled=True),
    )
    group_rows = image_block.shape[0]
    cycle_size = lax.axis_size("blk")
    cycle_place = lax.axis_index("blk")
    streams = [(1, 0, (image_block, text_block, owner_ids))]
    for cycle_step in range(cycle_size):
        next_streams = []
        for direction, offset, held_rows in streams:
            anchor = jnp.remainder(cycle_place - direction * cycle_step, cycle_size)
            absorb_text_block = held_rows[1]
            columns = (
                anchor * group_rows
                + offset
                + lax.broadcasted_iota(jnp.int32, (1, absorb_text_block.shape[0]), 1)
            )
            image_labels = (matched_caption_ids[:, None] == columns).astype(jnp.float32)
            text_labels = (text_index == held_rows[2][None, :]).astype(jnp.float32)
            image_part = weighted_sum(
                image_half, absorb_text_block, image_labels, sigmoid_multiplier, bias_value
            )
            text_part = weighted_sum(
                text_half, held_rows[0], text_labels, sigmoid_multiplier, bias_value
            )
            grads = (grads[0] + image_part, grads[1] + text_part)
            if cycle_step + 1 < cycle_size:
                held_rows = pass_on(held_rows, direction)
            next_streams.append((direction, offset, held_rows))
        streams = next_streams
    image_grad = back_through_norm(image_units, image_scale, grads[0])
    text_grad = back_through_norm(text_units, text_scale, grads[1])
    attn_grad = lax.dot_general(
        dense_result_adjoint,
        lax.all_gather(dense_mapping_matrix, "grp", axis=0, tiled=True),
        (((1,), (1,)), ((), ())),
        preferred_element_type=jnp.float32,
    ).astype(jnp.bfloat16)
    weight_share = lax.psum_scatter(
        lax.dot_general(
            heads_mixed_concluding,
            dense_result_adjoint,
            (((0,), (0,)), ((), ())),
            preferred_element_type=jnp.float32,
        ),
        "grp",
        scatter_dimension=0,
        tiled=True,
    )
    weight_total = lax.psum(weight_share, "blk")
    token_count = heads_mixed_concluding.shape[0] * lax.axis_size("blk") * lax.axis_size("grp")
    weight_grad = weight_total * (1.0 / math.sqrt(token_count))
    return (image_grad, text_grad, attn_grad, weight_grad)


MESH = pl.DeviceIdType.MESH
f32 = jnp.float32
bf16 = jnp.bfloat16


def fused_kernel(
    blks,
    zs,
    scale,
    sharp_ref,
    bias_ref,
    ids_ref,
    pic_hbm,
    cap_hbm,
    heads_hbm,
    adj_hbm,
    w_hbm,
    pic_out,
    cap_out,
    attn_out,
    wgrad_out,
    pic_ref,
    cap_ref,
    heads_ref,
    adj_ref,
    heads_t,
    heads_peer,
    adj_peer,
    w_full,
    part,
    first_in,
    second,
    second_in,
    zsum,
    zsum_in,
    done,
    img,
    img_ids,
    txt,
    img_part,
    img_core_in,
    img_z,
    img_z_in,
    txt_part,
    txt_in,
    load_sem,
    core_sem,
    wz_sem,
    w1_sem,
    w2_sem,
    wc_sem,
    first_sem,
    second_sem,
    zsum_sem,
    done_sem,
    iz_sem,
    tb_sem,
    ir_sem,
    tr_sem,
):
    b = lax.axis_index("blk")
    g = lax.axis_index("grp")
    z = g // 2
    c = g % 2
    rows, cols = w_hbm.shape
    chunk = rows // blks
    wide = 2 * rows
    own, width = pic_ref.shape
    flip = {1: b + 1 - 2 * lax.rem(b, 2), 2: lax.rem(b + 2, 4)}
    flip[3] = flip[1] + flip[2] - b

    def blk_peer(d):
        return (lax.rem(b + d, blks), g)

    def z_of(d):
        return lax.rem(z + zs + d, zs)

    def z_peer(d):
        return (b, z_of(d) * 2 + c)

    def rows_of(i):
        return pl.ds(pl.multiple_of(i * chunk, 16), chunk)

    partner = (b, z * 2 + 1 - c)
    mine = rows_of(b)

    def rcopy(src, dst, sems, to):
        return pltpu.make_async_remote_copy(
            src_ref=src, dst_ref=dst, send_sem=sems.at[0], recv_sem=sems.at[1],
            device_id=to, device_id_type=MESH,
        )

    sent = []

    def go(src, dst, sems, to):
        copy = rcopy(src, dst, sems, to)
        copy.start()
        sent.append(copy)

    def arrived(dst, sems):
        rcopy(dst, dst, sems, partner).wait_recv()

    barrier = pltpu.get_barrier_semaphore()
    peers = [blk_peer(d) for d in range(1, blks)] + [z_peer(d) for d in range(1, zs)] + [partner]
    for peer in peers:
        pl.semaphore_signal(barrier, inc=1, device_id=peer, device_id_type=MESH)
    loads = [
        pltpu.make_async_copy(src, dst, load_sem.at[i])
        for i, (src, dst) in enumerate(
            [
                (heads_hbm, heads_ref),
                (pic_hbm, pic_ref),
                (cap_hbm, cap_ref),
                (adj_hbm, adj_ref),
                (w_hbm, w_full.at[z, c]),
            ]
        )
    ]
    for load in loads:
        load.start()
    place = lax.broadcasted_iota(jnp.int32, (own, 128), 0)
    tile_ids = jnp.zeros((own, 128), jnp.int32)
    for i in range(own):
        tile_ids = jnp.where(place == i, ids_ref[i], tile_ids)
    img_ids[c, z] = tile_ids

    pl.semaphore_wait(barrier, len(peers))
    go(adj_hbm, adj_peer, core_sem.at[0], partner)
    for d in range(1, zs):
        go(w_hbm.at[mine], w_full.at[z, c, mine], wz_sem.at[d - 1], z_peer(d))

    loads[0].wait()
    for t in range(zs):
        turned = heads_ref[:, t * wide:(t + 1) * wide].T
        heads_t[0, t] = turned[:rows]
        heads_t[1, t] = turned[rows:]
    go(heads_t.at[1 - c], heads_peer, core_sem.at[1], partner)

    loads[1].wait()
    loads[2].wait()
    image_units, image_scale = unit_rows(pic_ref[...])
    text_units, text_scale = unit_rows(cap_ref[...])
    img[c, z] = image_units.astype(bf16)
    txt[b] = text_units.astype(bf16)
    for d in range(1, zs):
        go(img.at[c, z], img.at[c, z], iz_sem.at[d - 1, 0], z_peer(d))
        go(img_ids.at[c, z], img_ids.at[c, z], iz_sem.at[d - 1, 1], z_peer(d))
    for d in range(1, blks):
        go(txt.at[b], txt.at[b], tb_sem.at[d - 1], blk_peer(d))
    go(w_hbm, w_full.at[z, c], wc_sem.at[0], partner)

    loads[3].wait()
    arrived(adj_peer, core_sem.at[0])
    arrived(heads_peer, core_sem.at[1])
    tile = cols // 3 if cols % 384 == 0 else cols
    for k in range(zs):
        t = z_of(k + 1)
        for j in range(0, cols, tile):
            part[k, :, j:j + tile] = (
                jnp.dot(heads_t[c, t], adj_ref[:, j:j + tile], preferred_element_type=f32)
                + jnp.dot(heads_peer[t], adj_peer[:, j:j + tile], preferred_element_type=f32)
            ).astype(bf16)
        f = 1 + k % 2
        to = (flip[f], g)
        go(part.at[k, rows_of(flip[3])], first_in.at[k, 1], first_sem.at[k, 1], to)
        go(part.at[k, rows_of(flip[f])], first_in.at[k, 0], first_sem.at[k, 0], to)

    for d in range(1, zs):
        arrived(img.at[c, z_of(-d)], iz_sem.at[d - 1, 0])
        arrived(img_ids.at[c, z_of(-d)], iz_sem.at[d - 1, 1])
    go(img.at[c], img.at[c], core_sem.at[2], partner)
    go(img_ids.at[c], img_ids.at[c], core_sem.at[3], partner)

    half = cols // 2

    def w_piece(e, i, h):
        return w_full.at[z_of(-e), c, rows_of(i), h * half:(h + 1) * half]

    def w_first(e):
        arrived(w_full.at[z_of(-e), c, mine], wz_sem.at[e - 1])
        for h in range(2):
            piece = w_piece(e, b, h)
            go(piece, piece, w1_sem.at[e - 1, h], (flip[1 + h], g))

    def w_second(e):
        for h in range(2):
            got = w_piece(e, flip[1 + h], h)
            arrived(got, w1_sem.at[e - 1, h])
            to = (flip[2 - h], g)
            go(got, got, w2_sem.at[e - 1, h, 0], to)
            piece = w_piece(e, b, h)
            go(piece, piece, w2_sem.at[e - 1, h, 1], to)

    def w_core(e):
        for h in range(2):
            arrived(w_piece(e, flip[3], h), w2_sem.at[e - 1, h, 0])
            arrived(w_piece(e, flip[2 - h], h), w2_sem.at[e - 1, h, 1])
        block = w_full.at[z_of(-e), c]
        go(block, block, wc_sem.at[e], partner)

    def own_attn(e):
        zf = z_of(-e)
        arrived(w_full.at[zf, 1 - c], wc_sem.at[e])
        both = w_full[zf].reshape(wide, cols)
        attn_out[:, pl.ds(pl.multiple_of(zf * wide, 128), wide)] = lax.dot_general(
            adj_ref[...], both, (((1,), (1,)), ((), ())), preferred_element_type=f32
        ).astype(bf16)

    def step_two(k):
        s = 2 - k % 2
        arrived(first_in.at[k, 1], first_sem.at[k, 1])
        second[k] = (
            part[k, rows_of(flip[s])].astype(f32) + first_in[k, 1].astype(f32)
        ).astype(bf16)
        go(second.at[k], second_in.at[k], second_sem.at[k], (flip[s], g))

    def step_three(k):
        arrived(first_in.at[k, 0], first_sem.at[k, 0])
        arrived(second_in.at[k], second_sem.at[k])
        total = (
            part[k, mine].astype(f32) + first_in[k, 0].astype(f32) + second_in[k].astype(f32)
        )
        if k < zs - 1:
            zsum[k] = total.astype(bf16)
            go(zsum.at[k], zsum_in.at[k], zsum_sem.at[k], z_peer(k + 1))
        return total

    loads[4].wait()
    own_attn(0)

    for d in range(1, blks):
        arrived(txt.at[lax.rem(b + blks - d, blks)], tb_sem.at[d - 1])
    arrived(img.at[1 - c], core_sem.at[2])
    arrived(img_ids.at[1 - c], core_sem.at[3])
    image_rows = 2 * zs * own
    text_rows = blks * own
    images = img[...].reshape(image_rows, width)
    texts = txt[...].reshape(text_rows, width)
    owners = img_ids[...].reshape(image_rows, 128)[:, :1]
    lane = lax.broadcasted_iota(jnp.int32, (image_rows, text_rows), 1)
    column = ((lane // own) * (2 * zs) + g) * own + lane % own
    labels = (owners == column).astype(f32)
    inner_dots = lax.dot_general(
        images, texts, (((1,), (1,)), ((), ())), preferred_element_type=f32
    )
    sharp = sharp_ref[0]
    pair = sharp * (jax.nn.sigmoid(sharp * inner_dots + bias_ref[0]) - labels)
    img_part[...] = jnp.dot(pair.astype(bf16), texts, preferred_element_type=f32).reshape(
        2, zs, own, width
    )
    txt_part[...] = jnp.dot(
        pair.T.astype(bf16), images, preferred_element_type=f32
    ).reshape(blks, own, width)
    go(img_part.at[1 - c], img_core_in, core_sem.at[4], partner)
    for d in range(1, blks):
        to = blk_peer(d)
        go(txt_part.at[to[0]], txt_in.at[d - 1], tr_sem.at[d - 1], to)

    w_first(1)
    step_two(0)
    step_two(1)
    for e in range(2, zs):
        w_first(e)
        step_two(e)
    arrived(img_core_in, core_sem.at[4])
    img_z[...] = img_part[c] + img_core_in[...]
    for d in range(1, zs):
        go(img_z.at[z_of(d)], img_z_in.at[d - 1], ir_sem.at[d - 1], z_peer(d))
    for k in range(zs):
        total = step_three(k)
        if 1 <= k:
            w_second(k)

    for k in range(zs - 1):
        arrived(zsum_in.at[k], zsum_sem.at[k])
        total += zsum_in[k].astype(f32)
    done[0] = (total * scale).astype(bf16)
    for d in range(1, blks):
        go(done.at[0], done.at[d], done_sem.at[d - 1], blk_peer(d))

    for e in range(1, zs):
        w_core(e)
        if e > 1:
            own_attn(e - 1)

    image_grad = img_z[z]
    for d in range(1, zs):
        arrived(img_z_in.at[d - 1], ir_sem.at[d - 1])
        image_grad += img_z_in[d - 1]
    pic_out[...] = back_through_norm(image_units, image_scale, image_grad)
    text_grad = txt_part[b]
    for d in range(1, blks):
        arrived(txt_in.at[d - 1], tr_sem.at[d - 1])
        text_grad += txt_in[d - 1]
    cap_out[...] = back_through_norm(text_units, text_scale, text_grad)

    own_attn(zs - 1)
    wgrad_out[mine] = done[0].astype(f32)
    for d in range(1, blks):
        arrived(done.at[d], done_sem.at[d - 1])
        wgrad_out[rows_of(lax.rem(b + blks - d, blks))] = done[d].astype(f32)

    for copy in sent:
        copy.wait_send()


def fused_device(blks, grps, pic, cap, ids, sharp, bias, heads, adj, w):
    zs = grps // 2
    own, width = pic.shape
    tokens, cols = adj.shape
    rows = w.shape[0]
    chunk = rows // blks
    scale = 1.0 / math.sqrt(tokens * blks * grps)
    vmem = pl.BlockSpec(memory_space=pltpu.VMEM)
    smem = pl.BlockSpec(memory_space=pltpu.SMEM)
    hbm = pl.BlockSpec(memory_space=pl.ANY)
    dma = pltpu.SemaphoreType.DMA
    return pl.pallas_call(
        functools.partial(fused_kernel, blks, zs, scale),
        out_shape=(
            jax.ShapeDtypeStruct(pic.shape, f32),
            jax.ShapeDtypeStruct(cap.shape, f32),
            jax.ShapeDtypeStruct(heads.shape, bf16),
            jax.ShapeDtypeStruct(w.shape, f32),
        ),
        in_specs=[smem] * 3 + [hbm] * 5,
        out_specs=(vmem,) * 4,
        scratch_shapes=[
            pltpu.VMEM(pic.shape, f32),
            pltpu.VMEM(cap.shape, f32),
            pltpu.VMEM((tokens, cols), bf16),
            pltpu.VMEM((tokens, cols), bf16),
            pltpu.VMEM((2, zs, rows, tokens), bf16),
            pltpu.VMEM((zs, rows, tokens), bf16),
            pltpu.VMEM((tokens, cols), bf16),
            pltpu.VMEM((zs, 2, rows, cols), bf16),
            pltpu.VMEM((zs, rows, cols), bf16),
            pltpu.VMEM((zs, 2, chunk, cols), bf16),
            pltpu.VMEM((zs, chunk, cols), bf16),
            pltpu.VMEM((zs, chunk, cols), bf16),
            pltpu.VMEM((zs - 1, chunk, cols), bf16),
            pltpu.VMEM((zs - 1, chunk, cols), bf16),
            pltpu.VMEM((blks, chunk, cols), bf16),
            pltpu.VMEM((2, zs, own, width), bf16),
            pltpu.VMEM((2, zs, own, 128), jnp.int32),
            pltpu.VMEM((blks, own, width), bf16),
            pltpu.VMEM((2, zs, own, width), f32),
            pltpu.VMEM((zs, own, width), f32),
            pltpu.VMEM((zs, own, width), f32),
            pltpu.VMEM((zs - 1, own, width), f32),
            pltpu.VMEM((blks, own, width), f32),
            pltpu.VMEM((blks - 1, own, width), f32),
            dma((5,)),
            dma((5, 2)),
            dma((zs - 1, 2)),
            dma((zs - 1, 2, 2)),
            dma((zs - 1, 2, 2, 2)),
            dma((zs, 2)),
            dma((zs, 2, 2)),
            dma((zs, 2)),
            dma((zs - 1, 2)),
            dma((blks - 1, 2)),
            dma((zs - 1, 2, 2)),
            dma((blks - 1, 2)),
            dma((zs - 1, 2)),
            dma((blks - 1, 2)),
        ],
        compiler_params=pltpu.CompilerParams(
            collective_id=0, has_side_effects=True, vmem_limit_bytes=56 * 1024 * 1024
        ),
        cost_estimate=pl.CostEstimate(
            flops=4 * tokens * cols * cols, bytes_accessed=8 * tokens * cols, transcendentals=0
        ),
    )(sharp, bias, ids, pic, cap, heads, adj, w)


def per_device(pic, cap, ids, sharp, bias, heads, adj, w):
    blks = lax.axis_size("blk")
    grps = lax.axis_size("grp")
    own = pic.shape[0]
    rows, cols = w.shape
    fits = (
        grps % 2 == 0
        and grps >= 4
        and blks == 4
        and rows % (16 * blks) == 0
        and (2 * rows) % 128 == 0
        and heads.shape[1] == rows * grps
        and cols == heads.shape[1]
        and own % 16 == 0
        and cols % 256 == 0
    )
    if not fits:
        return plain_device(pic, cap, ids, sharp, bias, heads, adj, w)
    return fused_device(blks, grps, pic, cap, ids, sharp, bias, heads, adj, w)


def solution(mesh):
    placed = (
        P(("blk", "grp"), None),
        P(("blk", "grp"), None),
        P(("blk", "grp")),
        P(),
        P(),
        P(("blk", "grp"), None),
        P(("blk", "grp"), None),
        P("grp", None),
    )
    return jax.shard_map(
        per_device,
        mesh=mesh,
        in_specs=placed,
        out_specs=(
            P(("blk", "grp"), None),
            P(("blk", "grp"), None),
            P(("blk", "grp"), None),
            P("grp", None),
        ),
        check_vma=False,
    )
```

```python
import functools
import math

import jax
import jax.numpy as jnp
from jax import lax
from jax.experimental import pallas as pl
from jax.experimental.pallas import tpu as pltpu
from jax.sharding import PartitionSpec as P

stability_floor = 1e-06


def as_sent(x):

    def short(part):
        return part.astype(jnp.bfloat16) if part.dtype == jnp.float32 else part

    return jax.tree.map(short, x)


def passed_along(x, axis, by):
    peers = lax.axis_size(axis)
    return lax.ppermute(x, axis, [(i, (i + by) % peers) for i in range(peers)])


def unit_rows(raw):
    row_scale = lax.rsqrt(jnp.sum(raw * raw, axis=1, keepdims=True) + stability_floor)
    return (raw * row_scale, row_scale)


def back_through_norm(normed, row_scale, row_grad):
    along_unit = jnp.sum(normed * row_grad, axis=1, keepdims=True)
    return (row_grad - normed * along_unit) * row_scale


def weighted_sum(query_half, key_half, labels, sigmoid_multiplier, bias_value):
    inner_dots = lax.dot_general(
        query_half, key_half, (((1,), (1,)), ((), ())), preferred_element_type=jnp.float32
    )
    logits = sigmoid_multiplier * inner_dots + bias_value
    pair_weights = (sigmoid_multiplier * (jax.nn.sigmoid(logits) - labels)).astype(jnp.bfloat16)
    return jnp.dot(pair_weights, key_half, preferred_element_type=jnp.float32)


def pass_on(held_rows, direction):
    return jax.tree.map(
        lambda part, own: part.astype(own.dtype),
        passed_along(as_sent(held_rows), "blk", direction),
        held_rows,
    )


def plain_device(
    picture_vectors_prenorm,
    caption_vectors_prenorm,
    matched_caption_ids,
    sharpness_coefficient,
    additive_offset_term,
    heads_mixed_concluding,
    dense_result_adjoint,
    dense_mapping_matrix,
):
    image_units, image_scale = unit_rows(picture_vectors_prenorm)
    text_units, text_scale = unit_rows(caption_vectors_prenorm)
    image_half = image_units.astype(jnp.bfloat16)
    text_half = text_units.astype(jnp.bfloat16)
    sigmoid_multiplier = sharpness_coefficient[0]
    bias_value = additive_offset_term[0]
    own_rows = image_half.shape[0]
    own_first = (lax.axis_index("blk") * lax.axis_size("grp") + lax.axis_index("grp")) * own_rows
    text_index = own_first + lax.broadcasted_iota(jnp.int32, (own_rows, 1), 0)
    grads = (jnp.zeros(image_units.shape, jnp.float32), jnp.zeros(text_units.shape, jnp.float32))
    image_block, text_block, owner_ids = (
        lax.all_gather(image_half, "grp", axis=0, tiled=True),
        lax.all_gather(text_half, "grp", axis=0, tiled=True),
        lax.all_gather(matched_caption_ids, "grp", axis=0, tiled=True),
    )
    group_rows = image_block.shape[0]
    cycle_size = lax.axis_size("blk")
    cycle_place = lax.axis_index("blk")
    streams = [(1, 0, (image_block, text_block, owner_ids))]
    for cycle_step in range(cycle_size):
        next_streams = []
        for direction, offset, held_rows in streams:
            anchor = jnp.remainder(cycle_place - direction * cycle_step, cycle_size)
            absorb_text_block = held_rows[1]
            columns = (
                anchor * group_rows
                + offset
                + lax.broadcasted_iota(jnp.int32, (1, absorb_text_block.shape[0]), 1)
            )
            image_labels = (matched_caption_ids[:, None] == columns).astype(jnp.float32)
            text_labels = (text_index == held_rows[2][None, :]).astype(jnp.float32)
            image_part = weighted_sum(
                image_half, absorb_text_block, image_labels, sigmoid_multiplier, bias_value
            )
            text_part = weighted_sum(
                text_half, held_rows[0], text_labels, sigmoid_multiplier, bias_value
            )
            grads = (grads[0] + image_part, grads[1] + text_part)
            if cycle_step + 1 < cycle_size:
                held_rows = pass_on(held_rows, direction)
            next_streams.append((direction, offset, held_rows))
        streams = next_streams
    image_grad = back_through_norm(image_units, image_scale, grads[0])
    text_grad = back_through_norm(text_units, text_scale, grads[1])
    attn_grad = lax.dot_general(
        dense_result_adjoint,
        lax.all_gather(dense_mapping_matrix, "grp", axis=0, tiled=True),
        (((1,), (1,)), ((), ())),
        preferred_element_type=jnp.float32,
    ).astype(jnp.bfloat16)
    weight_share = lax.psum_scatter(
        lax.dot_general(
            heads_mixed_concluding,
            dense_result_adjoint,
            (((0,), (0,)), ((), ())),
            preferred_element_type=jnp.float32,
        ),
        "grp",
        scatter_dimension=0,
        tiled=True,
    )
    weight_total = lax.psum(weight_share, "blk")
    token_count = heads_mixed_concluding.shape[0] * lax.axis_size("blk") * lax.axis_size("grp")
    weight_grad = weight_total * (1.0 / math.sqrt(token_count))
    return (image_grad, text_grad, attn_grad, weight_grad)


MESH = pl.DeviceIdType.MESH
f32 = jnp.float32
bf16 = jnp.bfloat16


def fused_kernel(
    blks,
    zs,
    scale,
    sharp_ref,
    bias_ref,
    ids_ref,
    pic_hbm,
    cap_hbm,
    heads_hbm,
    adj_hbm,
    w_hbm,
    pic_out,
    cap_out,
    attn_out,
    wgrad_out,
    pic_ref,
    cap_ref,
    heads_ref,
    adj_ref,
    heads_t,
    heads_peer,
    adj_peer,
    w_full,
    part,
    first_in,
    second,
    second_in,
    zsum,
    zsum_in,
    done,
    img,
    img_ids,
    txt,
    img_part,
    img_core_in,
    img_z,
    img_z_in,
    txt_part,
    txt_in,
    load_sem,
    core_sem,
    wz_sem,
    w1_sem,
    w2_sem,
    wc_sem,
    first_sem,
    second_sem,
    zsum_sem,
    done_sem,
    iz_sem,
    tb_sem,
    ir_sem,
    tr_sem,
):
    b = lax.axis_index("blk")
    g = lax.axis_index("grp")
    z = g // 2
    c = g % 2
    rows, cols = w_hbm.shape
    chunk = rows // blks
    wide = 2 * rows
    own, width = pic_ref.shape
    flip = {1: b + 1 - 2 * lax.rem(b, 2), 2: lax.rem(b + 2, 4)}
    flip[3] = flip[1] + flip[2] - b

    def blk_peer(d):
        return (lax.rem(b + d, blks), g)

    def z_of(d):
        return lax.rem(z + zs + d, zs)

    def z_peer(d):
        return (b, z_of(d) * 2 + c)

    def rows_of(i):
        return pl.ds(pl.multiple_of(i * chunk, 16), chunk)

    partner = (b, z * 2 + 1 - c)
    mine = rows_of(b)

    def rcopy(src, dst, sems, to):
        return pltpu.make_async_remote_copy(
            src_ref=src, dst_ref=dst, send_sem=sems.at[0], recv_sem=sems.at[1],
            device_id=to, device_id_type=MESH,
        )

    sent = []

    def go(src, dst, sems, to):
        copy = rcopy(src, dst, sems, to)
        copy.start()
        sent.append(copy)

    def arrived(dst, sems):
        rcopy(dst, dst, sems, partner).wait_recv()

    barrier = pltpu.get_barrier_semaphore()
    peers = [blk_peer(d) for d in range(1, blks)] + [z_peer(d) for d in range(1, zs)] + [partner]
    for peer in peers:
        pl.semaphore_signal(barrier, inc=1, device_id=peer, device_id_type=MESH)
    loads = [
        pltpu.make_async_copy(src, dst, load_sem.at[i])
        for i, (src, dst) in enumerate(
            [
                (pic_hbm, pic_ref),
                (cap_hbm, cap_ref),
                (heads_hbm, heads_ref),
                (adj_hbm, adj_ref),
                (w_hbm, w_full.at[z, c]),
            ]
        )
    ]
    for load in loads:
        load.start()
    place = lax.broadcasted_iota(jnp.int32, (own, 128), 0)
    tile_ids = jnp.zeros((own, 128), jnp.int32)
    for i in range(own):
        tile_ids = jnp.where(place == i, ids_ref[i], tile_ids)
    img_ids[c, z] = tile_ids
    loads[0].wait()
    loads[1].wait()
    image_units, image_scale = unit_rows(pic_ref[...])
    text_units, text_scale = unit_rows(cap_ref[...])
    img[c, z] = image_units.astype(bf16)
    txt[b] = text_units.astype(bf16)

    pl.semaphore_wait(barrier, len(peers))
    go(adj_hbm, adj_peer, core_sem.at[0], partner)
    for d in range(1, zs):
        go(img.at[c, z], img.at[c, z], iz_sem.at[d - 1, 0], z_peer(d))
        go(img_ids.at[c, z], img_ids.at[c, z], iz_sem.at[d - 1, 1], z_peer(d))
    for d in range(1, blks):
        go(txt.at[b], txt.at[b], tb_sem.at[d - 1], blk_peer(d))
    for d in range(1, zs):
        go(w_hbm.at[mine], w_full.at[z, c, mine], wz_sem.at[d - 1], z_peer(d))

    loads[2].wait()
    for t in range(zs):
        turned = heads_ref[:, t * wide:(t + 1) * wide].T
        heads_t[0, t] = turned[:rows]
        heads_t[1, t] = turned[rows:]
    go(heads_t.at[1 - c], heads_peer, core_sem.at[1], partner)

    loads[3].wait()
    arrived(adj_peer, core_sem.at[0])
    arrived(heads_peer, core_sem.at[1])
    half = cols // 2
    for h in range(2):
        for k in range(zs):
            t = z_of(k + 1)
            for j in range(0, half, 256):
                at = h * half + j
                part[h, k, :, j:j + 256] = (
                    jnp.dot(heads_t[c, t], adj_ref[:, at:at + 256], preferred_element_type=f32)
                    + jnp.dot(heads_peer[t], adj_peer[:, at:at + 256], preferred_element_type=f32)
                ).astype(bf16)
            f = 1 + (h + k) % 2
            to = (flip[f], g)
            go(part.at[h, k, rows_of(flip[3])], first_in.at[h, k, 1], first_sem.at[h, k, 1], to)
            go(part.at[h, k, rows_of(flip[f])], first_in.at[h, k, 0], first_sem.at[h, k, 0], to)
    go(w_hbm, w_full.at[z, c], wc_sem.at[0], partner)

    for d in range(1, zs):
        arrived(img.at[c, z_of(-d)], iz_sem.at[d - 1, 0])
        arrived(img_ids.at[c, z_of(-d)], iz_sem.at[d - 1, 1])
    go(img.at[c], img.at[c], core_sem.at[2], partner)
    go(img_ids.at[c], img_ids.at[c], core_sem.at[3], partner)

    def w_piece(e, i, h):
        return w_full.at[z_of(-e), c, rows_of(i), h * half:(h + 1) * half]

    def w_first(e):
        arrived(w_full.at[z_of(-e), c, mine], wz_sem.at[e - 1])
        for h in range(2):
            piece = w_piece(e, b, h)
            go(piece, piece, w1_sem.at[e - 1, h], (flip[1 + h], g))

    def w_second(e):
        for h in range(2):
            got = w_piece(e, flip[1 + h], h)
            arrived(got, w1_sem.at[e - 1, h])
            to = (flip[2 - h], g)
            go(got, got, w2_sem.at[e - 1, h, 0], to)
            piece = w_piece(e, b, h)
            go(piece, piece, w2_sem.at[e - 1, h, 1], to)

    def w_core(e):
        for h in range(2):
            arrived(w_piece(e, flip[3], h), w2_sem.at[e - 1, h, 0])
            arrived(w_piece(e, flip[2 - h], h), w2_sem.at[e - 1, h, 1])
        block = w_full.at[z_of(-e), c]
        go(block, block, wc_sem.at[e], partner)

    def own_attn(e):
        zf = z_of(-e)
        arrived(w_full.at[zf, 1 - c], wc_sem.at[e])
        both = w_full[zf].reshape(wide, cols)
        attn_out[:, pl.ds(pl.multiple_of(zf * wide, 128), wide)] = lax.dot_general(
            adj_ref[...], both, (((1,), (1,)), ((), ())), preferred_element_type=f32
        ).astype(bf16)

    def step_two(h, k):
        s = 2 - (h + k) % 2
        arrived(first_in.at[h, k, 1], first_sem.at[h, k, 1])
        second[h, k] = (
            part[h, k, rows_of(flip[s])].astype(f32) + first_in[h, k, 1].astype(f32)
        ).astype(bf16)
        go(second.at[h, k], second_in.at[h, k], second_sem.at[h, k], (flip[s], g))

    def step_three(h, k):
        arrived(first_in.at[h, k, 0], first_sem.at[h, k, 0])
        arrived(second_in.at[h, k], second_sem.at[h, k])
        total = (
            part[h, k, mine].astype(f32)
            + first_in[h, k, 0].astype(f32)
            + second_in[h, k].astype(f32)
        )
        if k < zs - 1:
            zsum[h, k] = total.astype(bf16)
            go(zsum.at[h, k], zsum_in.at[h, k], zsum_sem.at[h, k], z_peer(k + 1))
        return total

    def finish(h, total):
        for k in range(zs - 1):
            arrived(zsum_in.at[h, k], zsum_sem.at[h, k])
            total += zsum_in[h, k].astype(f32)
        done[h, 0] = (total * scale).astype(bf16)
        for d in range(1, blks):
            go(done.at[h, 0], done.at[h, d], done_sem.at[h, d - 1], blk_peer(d))

    w_first(1)
    for k in range(zs):
        step_two(0, k)
    for e in range(2, zs):
        w_first(e)
    for k in range(zs):
        step_two(1, k)

    for d in range(1, blks):
        arrived(txt.at[lax.rem(b + blks - d, blks)], tb_sem.at[d - 1])
    arrived(img.at[1 - c], core_sem.at[2])
    arrived(img_ids.at[1 - c], core_sem.at[3])
    image_rows = 2 * zs * own
    text_rows = blks * own
    images = img[...].reshape(image_rows, width)
    texts = txt[...].reshape(text_rows, width)
    owners = img_ids[...].reshape(image_rows, 128)[:, :1]
    lane = lax.broadcasted_iota(jnp.int32, (image_rows, text_rows), 1)
    column = ((lane // own) * (2 * zs) + g) * own + lane % own
    labels = (owners == column).astype(f32)
    inner_dots = lax.dot_general(
        images, texts, (((1,), (1,)), ((), ())), preferred_element_type=f32
    )
    sharp = sharp_ref[0]
    pair = sharp * (jax.nn.sigmoid(sharp * inner_dots + bias_ref[0]) - labels)
    img_part[...] = jnp.dot(pair.astype(bf16), texts, preferred_element_type=f32).reshape(
        2, zs, own, width
    )
    txt_part[...] = jnp.dot(
        pair.T.astype(bf16), images, preferred_element_type=f32
    ).reshape(blks, own, width)
    go(img_part.at[1 - c], img_core_in, core_sem.at[4], partner)
    for d in range(1, blks):
        to = blk_peer(d)
        go(txt_part.at[to[0]], txt_in.at[d - 1], tr_sem.at[d - 1], to)

    for k in range(zs):
        total_a = step_three(0, k)
        if k == 1:
            w_second(1)
    arrived(img_core_in, core_sem.at[4])
    img_z[...] = img_part[c] + img_core_in[...]
    for d in range(1, zs):
        go(img_z.at[z_of(d)], img_z_in.at[d - 1], ir_sem.at[d - 1], z_peer(d))
    for k in range(zs):
        total_b = step_three(1, k)
        if 1 < k:
            w_second(k)
    loads[4].wait()
    own_attn(0)

    finish(0, total_a)
    w_core(1)
    finish(1, total_b)
    for e in range(2, zs):
        w_core(e)
        own_attn(e - 1)

    image_grad = img_z[z]
    for d in range(1, zs):
        arrived(img_z_in.at[d - 1], ir_sem.at[d - 1])
        image_grad += img_z_in[d - 1]
    pic_out[...] = back_through_norm(image_units, image_scale, image_grad)
    text_grad = txt_part[b]
    for d in range(1, blks):
        arrived(txt_in.at[d - 1], tr_sem.at[d - 1])
        text_grad += txt_in[d - 1]
    cap_out[...] = back_through_norm(text_units, text_scale, text_grad)

    own_attn(zs - 1)
    for h in range(2):
        span = slice(h * half, (h + 1) * half)
        wgrad_out[mine, span] = done[h, 0].astype(f32)
        for d in range(1, blks):
            arrived(done.at[h, d], done_sem.at[h, d - 1])
            wgrad_out[rows_of(lax.rem(b + blks - d, blks)), span] = done[h, d].astype(f32)

    for copy in sent:
        copy.wait_send()


def store_kernel(*refs):
    copies = [pltpu.make_async_copy(refs[i], refs[4 + i], refs[8].at[i]) for i in range(4)]
    for copy in copies:
        copy.start()
    for copy in copies:
        copy.wait()


def fused_device(blks, grps, pic, cap, ids, sharp, bias, heads, adj, w):
    zs = grps // 2
    own, width = pic.shape
    tokens, cols = adj.shape
    rows = w.shape[0]
    chunk = rows // blks
    half = cols // 2
    scale = 1.0 / math.sqrt(tokens * blks * grps)
    vmem = pl.BlockSpec(memory_space=pltpu.VMEM)
    smem = pl.BlockSpec(memory_space=pltpu.SMEM)
    hbm = pl.BlockSpec(memory_space=pltpu.HBM)
    dma = pltpu.SemaphoreType.DMA
    grads = pl.pallas_call(
        functools.partial(fused_kernel, blks, zs, scale),
        out_shape=(
            jax.ShapeDtypeStruct(pic.shape, f32),
            jax.ShapeDtypeStruct(cap.shape, f32),
            jax.ShapeDtypeStruct(heads.shape, bf16),
            jax.ShapeDtypeStruct(w.shape, f32),
        ),
        in_specs=[smem] * 3 + [hbm] * 5,
        out_specs=(vmem,) * 4,
        scratch_shapes=[
            pltpu.VMEM(pic.shape, f32),
            pltpu.VMEM(cap.shape, f32),
            pltpu.VMEM((tokens, cols), bf16),
            pltpu.VMEM((tokens, cols), bf16),
            pltpu.VMEM((2, zs, rows, tokens), bf16),
            pltpu.VMEM((zs, rows, tokens), bf16),
            pltpu.VMEM((tokens, cols), bf16),
            pltpu.VMEM((zs, 2, rows, cols), bf16),
            pltpu.VMEM((2, zs, rows, half), bf16),
            pltpu.VMEM((2, zs, 2, chunk, half), bf16),
            pltpu.VMEM((2, zs, chunk, half), bf16),
            pltpu.VMEM((2, zs, chunk, half), bf16),
            pltpu.VMEM((2, zs - 1, chunk, half), bf16),
            pltpu.VMEM((2, zs - 1, chunk, half), bf16),
            pltpu.VMEM((2, blks, chunk, half), bf16),
            pltpu.VMEM((2, zs, own, width), bf16),
            pltpu.VMEM((2, zs, own, 128), jnp.int32),
            pltpu.VMEM((blks, own, width), bf16),
            pltpu.VMEM((2, zs, own, width), f32),
            pltpu.VMEM((zs, own, width), f32),
            pltpu.VMEM((zs, own, width), f32),
            pltpu.VMEM((zs - 1, own, width), f32),
            pltpu.VMEM((blks, own, width), f32),
            pltpu.VMEM((blks - 1, own, width), f32),
            dma((5,)),
            dma((5, 2)),
            dma((zs - 1, 2)),
            dma((zs - 1, 2, 2)),
            dma((zs - 1, 2, 2, 2)),
            dma((zs, 2)),
            dma((2, zs, 2, 2)),
            dma((2, zs, 2)),
            dma((2, zs - 1, 2)),
            dma((2, blks - 1, 2)),
            dma((zs - 1, 2, 2)),
            dma((blks - 1, 2)),
            dma((zs - 1, 2)),
            dma((blks - 1, 2)),
        ],
        compiler_params=pltpu.CompilerParams(
            collective_id=0, has_side_effects=True, vmem_limit_bytes=50 * 1024 * 1024
        ),
        cost_estimate=pl.CostEstimate(
            flops=4 * tokens * cols * cols, bytes_accessed=8 * tokens * cols, transcendentals=0
        ),
    )(sharp, bias, ids, pic, cap, heads, adj, w)
    anywhere = pl.BlockSpec(memory_space=pl.ANY)
    return pl.pallas_call(
        store_kernel,
        out_shape=tuple(jax.ShapeDtypeStruct(x.shape, x.dtype) for x in grads),
        in_specs=[anywhere] * 4,
        out_specs=(anywhere,) * 4,
        scratch_shapes=[dma((4,))],
    )(*grads)


def per_device(pic, cap, ids, sharp, bias, heads, adj, w):
    blks = lax.axis_size("blk")
    grps = lax.axis_size("grp")
    own = pic.shape[0]
    rows, cols = w.shape
    fits = (
        grps % 2 == 0
        and grps >= 4
        and blks == 4
        and rows % (16 * blks) == 0
        and (2 * rows) % 128 == 0
        and heads.shape[1] == rows * grps
        and cols == heads.shape[1]
        and own % 16 == 0
        and cols % 512 == 0
    )
    if not fits:
        return plain_device(pic, cap, ids, sharp, bias, heads, adj, w)
    return fused_device(blks, grps, pic, cap, ids, sharp, bias, heads, adj, w)


def solution(mesh):
    placed = (
        P(("blk", "grp"), None),
        P(("blk", "grp"), None),
        P(("blk", "grp")),
        P(),
        P(),
        P(("blk", "grp"), None),
        P(("blk", "grp"), None),
        P("grp", None),
    )
    return jax.shard_map(
        per_device,
        mesh=mesh,
        in_specs=placed,
        out_specs=(
            P(("blk", "grp"), None),
            P(("blk", "grp"), None),
            P(("blk", "grp"), None),
            P("grp", None),
        ),
        check_vma=False,
    )
```

```python
import functools
import math

import jax
import jax.numpy as jnp
from jax import lax
from jax.experimental import pallas as pl
from jax.experimental.pallas import tpu as pltpu
from jax.sharding import PartitionSpec as P

stability_floor = 1e-06


def as_sent(x):

    def short(part):
        return part.astype(jnp.bfloat16) if part.dtype == jnp.float32 else part

    return jax.tree.map(short, x)


def passed_along(x, axis, by):
    peers = lax.axis_size(axis)
    return lax.ppermute(x, axis, [(i, (i + by) % peers) for i in range(peers)])


def unit_rows(raw):
    row_scale = lax.rsqrt(jnp.sum(raw * raw, axis=1, keepdims=True) + stability_floor)
    return (raw * row_scale, row_scale)


def back_through_norm(normed, row_scale, row_grad):
    along_unit = jnp.sum(normed * row_grad, axis=1, keepdims=True)
    return (row_grad - normed * along_unit) * row_scale


def weighted_sum(query_half, key_half, labels, sigmoid_multiplier, bias_value):
    inner_dots = lax.dot_general(
        query_half, key_half, (((1,), (1,)), ((), ())), preferred_element_type=jnp.float32
    )
    logits = sigmoid_multiplier * inner_dots + bias_value
    pair_weights = (sigmoid_multiplier * (jax.nn.sigmoid(logits) - labels)).astype(jnp.bfloat16)
    return jnp.dot(pair_weights, key_half, preferred_element_type=jnp.float32)


def pass_on(held_rows, direction):
    return jax.tree.map(
        lambda part, own: part.astype(own.dtype),
        passed_along(as_sent(held_rows), "blk", direction),
        held_rows,
    )


def plain_device(
    picture_vectors_prenorm,
    caption_vectors_prenorm,
    matched_caption_ids,
    sharpness_coefficient,
    additive_offset_term,
    heads_mixed_concluding,
    dense_result_adjoint,
    dense_mapping_matrix,
):
    image_units, image_scale = unit_rows(picture_vectors_prenorm)
    text_units, text_scale = unit_rows(caption_vectors_prenorm)
    image_half = image_units.astype(jnp.bfloat16)
    text_half = text_units.astype(jnp.bfloat16)
    sigmoid_multiplier = sharpness_coefficient[0]
    bias_value = additive_offset_term[0]
    own_rows = image_half.shape[0]
    own_first = (lax.axis_index("blk") * lax.axis_size("grp") + lax.axis_index("grp")) * own_rows
    text_index = own_first + lax.broadcasted_iota(jnp.int32, (own_rows, 1), 0)
    grads = (jnp.zeros(image_units.shape, jnp.float32), jnp.zeros(text_units.shape, jnp.float32))
    image_block, text_block, owner_ids = (
        lax.all_gather(image_half, "grp", axis=0, tiled=True),
        lax.all_gather(text_half, "grp", axis=0, tiled=True),
        lax.all_gather(matched_caption_ids, "grp", axis=0, tiled=True),
    )
    group_rows = image_block.shape[0]
    cycle_size = lax.axis_size("blk")
    cycle_place = lax.axis_index("blk")
    streams = [(1, 0, (image_block, text_block, owner_ids))]
    for cycle_step in range(cycle_size):
        next_streams = []
        for direction, offset, held_rows in streams:
            anchor = jnp.remainder(cycle_place - direction * cycle_step, cycle_size)
            absorb_text_block = held_rows[1]
            columns = (
                anchor * group_rows
                + offset
                + lax.broadcasted_iota(jnp.int32, (1, absorb_text_block.shape[0]), 1)
            )
            image_labels = (matched_caption_ids[:, None] == columns).astype(jnp.float32)
            text_labels = (text_index == held_rows[2][None, :]).astype(jnp.float32)
            image_part = weighted_sum(
                image_half, absorb_text_block, image_labels, sigmoid_multiplier, bias_value
            )
            text_part = weighted_sum(
                text_half, held_rows[0], text_labels, sigmoid_multiplier, bias_value
            )
            grads = (grads[0] + image_part, grads[1] + text_part)
            if cycle_step + 1 < cycle_size:
                held_rows = pass_on(held_rows, direction)
            next_streams.append((direction, offset, held_rows))
        streams = next_streams
    image_grad = back_through_norm(image_units, image_scale, grads[0])
    text_grad = back_through_norm(text_units, text_scale, grads[1])
    attn_grad = lax.dot_general(
        dense_result_adjoint,
        lax.all_gather(dense_mapping_matrix, "grp", axis=0, tiled=True),
        (((1,), (1,)), ((), ())),
        preferred_element_type=jnp.float32,
    ).astype(jnp.bfloat16)
    weight_share = lax.psum_scatter(
        lax.dot_general(
            heads_mixed_concluding,
            dense_result_adjoint,
            (((0,), (0,)), ((), ())),
            preferred_element_type=jnp.float32,
        ),
        "grp",
        scatter_dimension=0,
        tiled=True,
    )
    weight_total = lax.psum(weight_share, "blk")
    token_count = heads_mixed_concluding.shape[0] * lax.axis_size("blk") * lax.axis_size("grp")
    weight_grad = weight_total * (1.0 / math.sqrt(token_count))
    return (image_grad, text_grad, attn_grad, weight_grad)


MESH = pl.DeviceIdType.MESH
f32 = jnp.float32
bf16 = jnp.bfloat16


def fused_kernel(
    blks,
    zs,
    scale,
    sharp_ref,
    bias_ref,
    ids_ref,
    pic_hbm,
    cap_hbm,
    heads_hbm,
    adj_hbm,
    w_hbm,
    pic_out,
    cap_out,
    attn_out,
    wgrad_out,
    pic_ref,
    cap_ref,
    heads_ref,
    adj_ref,
    heads_t,
    heads_peer,
    adj_peer,
    w_full,
    part,
    first_in,
    second,
    second_in,
    zsum,
    zsum_in,
    done,
    img,
    img_ids,
    txt,
    img_part,
    img_core_in,
    img_z,
    img_z_in,
    txt_part,
    txt_in,
    load_sem,
    core_sem,
    turn_sem,
    wz_sem,
    w1_sem,
    w2_sem,
    wc_sem,
    first_sem,
    second_sem,
    zsum_sem,
    done_sem,
    iz_sem,
    tb_sem,
    ir_sem,
    tr_sem,
):
    b = lax.axis_index("blk")
    g = lax.axis_index("grp")
    z = g // 2
    c = g % 2
    rows, cols = w_hbm.shape
    chunk = rows // blks
    wide = 2 * rows
    own, width = pic_ref.shape
    flip = {1: b + 1 - 2 * lax.rem(b, 2), 2: lax.rem(b + 2, 4)}
    flip[3] = flip[1] + flip[2] - b

    def blk_peer(d):
        return (lax.rem(b + d, blks), g)

    def z_of(d):
        return lax.rem(z + zs + d, zs)

    def z_peer(d):
        return (b, z_of(d) * 2 + c)

    def rows_of(i):
        return pl.ds(pl.multiple_of(i * chunk, 16), chunk)

    partner = (b, z * 2 + 1 - c)
    mine = rows_of(b)

    def rcopy(src, dst, sems, to):
        return pltpu.make_async_remote_copy(
            src_ref=src, dst_ref=dst, send_sem=sems.at[0], recv_sem=sems.at[1],
            device_id=to, device_id_type=MESH,
        )

    sent = []

    def go(src, dst, sems, to):
        copy = rcopy(src, dst, sems, to)
        copy.start()
        sent.append(copy)

    def arrived(dst, sems):
        rcopy(dst, dst, sems, partner).wait_recv()

    barrier = pltpu.get_barrier_semaphore()
    peers = [blk_peer(d) for d in range(1, blks)] + [z_peer(d) for d in range(1, zs)] + [partner]
    for peer in peers:
        pl.semaphore_signal(barrier, inc=1, device_id=peer, device_id_type=MESH)
    loads = [
        pltpu.make_async_copy(src, dst, load_sem.at[i])
        for i, (src, dst) in enumerate(
            [
                (pic_hbm, pic_ref),
                (cap_hbm, cap_ref),
                (heads_hbm, heads_ref),
                (adj_hbm, adj_ref),
                (w_hbm, w_full.at[z, c]),
            ]
        )
    ]
    for load in loads:
        load.start()
    place = lax.broadcasted_iota(jnp.int32, (own, 128), 0)
    tile_ids = jnp.zeros((own, 128), jnp.int32)
    for i in range(own):
        tile_ids = jnp.where(place == i, ids_ref[i], tile_ids)
    img_ids[c, z] = tile_ids
    loads[0].wait()
    loads[1].wait()
    image_units, image_scale = unit_rows(pic_ref[...])
    text_units, text_scale = unit_rows(cap_ref[...])
    img[c, z] = image_units.astype(bf16)
    txt[b] = text_units.astype(bf16)

    pl.semaphore_wait(barrier, len(peers))
    go(adj_hbm, adj_peer, core_sem.at[0], partner)
    for d in range(1, zs):
        go(img.at[c, z], img.at[c, z], iz_sem.at[d - 1, 0], z_peer(d))
        go(img_ids.at[c, z], img_ids.at[c, z], iz_sem.at[d - 1, 1], z_peer(d))
    for d in range(1, blks):
        go(txt.at[b], txt.at[b], tb_sem.at[d - 1], blk_peer(d))
    for d in range(1, zs):
        go(w_hbm.at[mine], w_full.at[z, c, mine], wz_sem.at[d - 1], z_peer(d))

    loads[2].wait()
    for k in range(zs):
        t = z_of(k + 1)
        turned = heads_ref[:, pl.ds(pl.multiple_of(t * wide, 128), wide)].T
        heads_t[0, k] = turned[:rows]
        heads_t[1, k] = turned[rows:]
        go(heads_t.at[1 - c, k], heads_peer.at[k], turn_sem.at[k], partner)

    loads[3].wait()
    arrived(adj_peer, core_sem.at[0])
    half = cols // 2
    for h in range(2):
        for k in range(zs):
            if h == 0:
                arrived(heads_peer.at[k], turn_sem.at[k])
            for j in range(0, half, 256):
                at = h * half + j
                part[h, k, :, j:j + 256] = (
                    jnp.dot(heads_t[c, k], adj_ref[:, at:at + 256], preferred_element_type=f32)
                    + jnp.dot(heads_peer[k], adj_peer[:, at:at + 256], preferred_element_type=f32)
                ).astype(bf16)
            f = 1 + (h + k) % 2
            to = (flip[f], g)
            go(part.at[h, k, rows_of(flip[3])], first_in.at[h, k, 1], first_sem.at[h, k, 1], to)
            go(part.at[h, k, rows_of(flip[f])], first_in.at[h, k, 0], first_sem.at[h, k, 0], to)
    go(w_hbm, w_full.at[z, c], wc_sem.at[0], partner)

    for d in range(1, zs):
        arrived(img.at[c, z_of(-d)], iz_sem.at[d - 1, 0])
        arrived(img_ids.at[c, z_of(-d)], iz_sem.at[d - 1, 1])
    go(img.at[c], img.at[c], core_sem.at[2], partner)
    go(img_ids.at[c], img_ids.at[c], core_sem.at[3], partner)

    def w_piece(e, i, h):
        return w_full.at[z_of(-e), c, rows_of(i), h * half:(h + 1) * half]

    def w_first(e):
        arrived(w_full.at[z_of(-e), c, mine], wz_sem.at[e - 1])
        for h in range(2):
            piece = w_piece(e, b, h)
            go(piece, piece, w1_sem.at[e - 1, h], (flip[1 + h], g))

    def w_second(e):
        for h in range(2):
            got = w_piece(e, flip[1 + h], h)
            arrived(got, w1_sem.at[e - 1, h])
            to = (flip[2 - h], g)
            go(got, got, w2_sem.at[e - 1, h, 0], to)
            piece = w_piece(e, b, h)
            go(piece, piece, w2_sem.at[e - 1, h, 1], to)

    def w_core(e):
        for h in range(2):
            arrived(w_piece(e, flip[3], h), w2_sem.at[e - 1, h, 0])
            arrived(w_piece(e, flip[2 - h], h), w2_sem.at[e - 1, h, 1])
        block = w_full.at[z_of(-e), c]
        go(block, block, wc_sem.at[e], partner)

    def own_attn(e):
        zf = z_of(-e)
        arrived(w_full.at[zf, 1 - c], wc_sem.at[e])
        both = w_full[zf].reshape(wide, cols)
        attn_out[:, pl.ds(pl.multiple_of(zf * wide, 128), wide)] = lax.dot_general(
            adj_ref[...], both, (((1,), (1,)), ((), ())), preferred_element_type=f32
        ).astype(bf16)

    def step_two(h, k):
        s = 2 - (h + k) % 2
        arrived(first_in.at[h, k, 1], first_sem.at[h, k, 1])
        second[h, k] = (
            part[h, k, rows_of(flip[s])].astype(f32) + first_in[h, k, 1].astype(f32)
        ).astype(bf16)
        go(second.at[h, k], second_in.at[h, k], second_sem.at[h, k], (flip[s], g))

    def step_three(h, k):
        arrived(first_in.at[h, k, 0], first_sem.at[h, k, 0])
        arrived(second_in.at[h, k], second_sem.at[h, k])
        total = (
            part[h, k, mine].astype(f32)
            + first_in[h, k, 0].astype(f32)
            + second_in[h, k].astype(f32)
        )
        if k < zs - 1:
            zsum[h, k] = total.astype(bf16)
            go(zsum.at[h, k], zsum_in.at[h, k], zsum_sem.at[h, k], z_peer(k + 1))
        return total

    def finish(h, total):
        for k in range(zs - 1):
            arrived(zsum_in.at[h, k], zsum_sem.at[h, k])
            total += zsum_in[h, k].astype(f32)
        done[h, 0] = (total * scale).astype(bf16)
        for d in range(1, blks):
            go(done.at[h, 0], done.at[h, d], done_sem.at[h, d - 1], blk_peer(d))

    w_first(1)
    for k in range(zs):
        step_two(0, k)
    for e in range(2, zs):
        w_first(e)
    for k in range(zs):
        step_two(1, k)

    for d in range(1, blks):
        arrived(txt.at[lax.rem(b + blks - d, blks)], tb_sem.at[d - 1])
    arrived(img.at[1 - c], core_sem.at[2])
    arrived(img_ids.at[1 - c], core_sem.at[3])
    image_rows = 2 * zs * own
    text_rows = blks * own
    images = img[...].reshape(image_rows, width)
    texts = txt[...].reshape(text_rows, width)
    owners = img_ids[...].reshape(image_rows, 128)[:, :1]
    lane = lax.broadcasted_iota(jnp.int32, (image_rows, text_rows), 1)
    column = ((lane // own) * (2 * zs) + g) * own + lane % own
    labels = (owners == column).astype(f32)
    inner_dots = lax.dot_general(
        images, texts, (((1,), (1,)), ((), ())), preferred_element_type=f32
    )
    sharp = sharp_ref[0]
    pair = sharp * (jax.nn.sigmoid(sharp * inner_dots + bias_ref[0]) - labels)
    img_part[...] = jnp.dot(pair.astype(bf16), texts, preferred_element_type=f32).reshape(
        2, zs, own, width
    )
    txt_part[...] = jnp.dot(
        pair.T.astype(bf16), images, preferred_element_type=f32
    ).reshape(blks, own, width)
    go(img_part.at[1 - c], img_core_in, core_sem.at[4], partner)
    for d in range(1, blks):
        to = blk_peer(d)
        go(txt_part.at[to[0]], txt_in.at[d - 1], tr_sem.at[d - 1], to)

    for k in range(zs):
        total_a = step_three(0, k)
        if k == 1:
            w_second(1)
    arrived(img_core_in, core_sem.at[4])
    img_z[...] = img_part[c] + img_core_in[...]
    for d in range(1, zs):
        go(img_z.at[z_of(d)], img_z_in.at[d - 1], ir_sem.at[d - 1], z_peer(d))
    for k in range(zs):
        total_b = step_three(1, k)
        if 1 < k:
            w_second(k)
    loads[4].wait()
    own_attn(0)

    finish(0, total_a)
    w_core(1)
    finish(1, total_b)
    for e in range(2, zs):
        w_core(e)
        own_attn(e - 1)

    image_grad = img_z[z]
    for d in range(1, zs):
        arrived(img_z_in.at[d - 1], ir_sem.at[d - 1])
        image_grad += img_z_in[d - 1]
    pic_out[...] = back_through_norm(image_units, image_scale, image_grad)
    text_grad = txt_part[b]
    for d in range(1, blks):
        arrived(txt_in.at[d - 1], tr_sem.at[d - 1])
        text_grad += txt_in[d - 1]
    cap_out[...] = back_through_norm(text_units, text_scale, text_grad)

    own_attn(zs - 1)
    for h in range(2):
        span = slice(h * half, (h + 1) * half)
        wgrad_out[mine, span] = done[h, 0].astype(f32)
        for d in range(1, blks):
            arrived(done.at[h, d], done_sem.at[h, d - 1])
            wgrad_out[rows_of(lax.rem(b + blks - d, blks)), span] = done[h, d].astype(f32)

    for copy in sent:
        copy.wait_send()


def store_kernel(*refs):
    for i in range(4):
        refs[4 + i][...] = refs[i][...]


def fused_device(blks, grps, pic, cap, ids, sharp, bias, heads, adj, w):
    zs = grps // 2
    own, width = pic.shape
    tokens, cols = adj.shape
    rows = w.shape[0]
    chunk = rows // blks
    half = cols // 2
    scale = 1.0 / math.sqrt(tokens * blks * grps)
    vmem = pl.BlockSpec(memory_space=pltpu.VMEM)
    smem = pl.BlockSpec(memory_space=pltpu.SMEM)
    hbm = pl.BlockSpec(memory_space=pltpu.HBM)
    dma = pltpu.SemaphoreType.DMA
    grads = pl.pallas_call(
        functools.partial(fused_kernel, blks, zs, scale),
        out_shape=(
            jax.ShapeDtypeStruct(pic.shape, f32),
            jax.ShapeDtypeStruct(cap.shape, f32),
            jax.ShapeDtypeStruct(heads.shape, bf16),
            jax.ShapeDtypeStruct(w.shape, f32),
        ),
        in_specs=[smem] * 3 + [hbm] * 5,
        out_specs=(vmem,) * 4,
        scratch_shapes=[
            pltpu.VMEM(pic.shape, f32),
            pltpu.VMEM(cap.shape, f32),
            pltpu.VMEM((tokens, cols), bf16),
            pltpu.VMEM((tokens, cols), bf16),
            pltpu.VMEM((2, zs, rows, tokens), bf16),
            pltpu.VMEM((zs, rows, tokens), bf16),
            pltpu.VMEM((tokens, cols), bf16),
            pltpu.VMEM((zs, 2, rows, cols), bf16),
            pltpu.VMEM((2, zs, rows, half), bf16),
            pltpu.VMEM((2, zs, 2, chunk, half), bf16),
            pltpu.VMEM((2, zs, chunk, half), bf16),
            pltpu.VMEM((2, zs, chunk, half), bf16),
            pltpu.VMEM((2, zs - 1, chunk, half), bf16),
            pltpu.VMEM((2, zs - 1, chunk, half), bf16),
            pltpu.VMEM((2, blks, chunk, half), bf16),
            pltpu.VMEM((2, zs, own, width), bf16),
            pltpu.VMEM((2, zs, own, 128), jnp.int32),
            pltpu.VMEM((blks, own, width), bf16),
            pltpu.VMEM((2, zs, own, width), f32),
            pltpu.VMEM((zs, own, width), f32),
            pltpu.VMEM((zs, own, width), f32),
            pltpu.VMEM((zs - 1, own, width), f32),
            pltpu.VMEM((blks, own, width), f32),
            pltpu.VMEM((blks - 1, own, width), f32),
            dma((5,)),
            dma((5, 2)),
            dma((zs, 2)),
            dma((zs - 1, 2)),
            dma((zs - 1, 2, 2)),
            dma((zs - 1, 2, 2, 2)),
            dma((zs, 2)),
            dma((2, zs, 2, 2)),
            dma((2, zs, 2)),
            dma((2, zs - 1, 2)),
            dma((2, blks - 1, 2)),
            dma((zs - 1, 2, 2)),
            dma((blks - 1, 2)),
            dma((zs - 1, 2)),
            dma((blks - 1, 2)),
        ],
        compiler_params=pltpu.CompilerParams(
            collective_id=0, has_side_effects=True, vmem_limit_bytes=50 * 1024 * 1024
        ),
        cost_estimate=pl.CostEstimate(
            flops=4 * tokens * cols * cols, bytes_accessed=8 * tokens * cols, transcendentals=0
        ),
    )(sharp, bias, ids, pic, cap, heads, adj, w)
    return pl.pallas_call(
        store_kernel,
        out_shape=tuple(jax.ShapeDtypeStruct(x.shape, x.dtype) for x in grads),
        in_specs=[vmem] * 4,
        out_specs=(vmem,) * 4,
    )(*grads)


def per_device(pic, cap, ids, sharp, bias, heads, adj, w):
    blks = lax.axis_size("blk")
    grps = lax.axis_size("grp")
    own = pic.shape[0]
    rows, cols = w.shape
    fits = (
        grps % 2 == 0
        and grps >= 4
        and blks == 4
        and rows % (16 * blks) == 0
        and (2 * rows) % 128 == 0
        and heads.shape[1] == rows * grps
        and cols == heads.shape[1]
        and own % 16 == 0
        and cols % 512 == 0
    )
    if not fits:
        return plain_device(pic, cap, ids, sharp, bias, heads, adj, w)
    return fused_device(blks, grps, pic, cap, ids, sharp, bias, heads, adj, w)


def solution(mesh):
    placed = (
        P(("blk", "grp"), None),
        P(("blk", "grp"), None),
        P(("blk", "grp")),
        P(),
        P(),
        P(("blk", "grp"), None),
        P(("blk", "grp"), None),
        P("grp", None),
    )
    return jax.shard_map(
        per_device,
        mesh=mesh,
        in_specs=placed,
        out_specs=(
            P(("blk", "grp"), None),
            P(("blk", "grp"), None),
            P(("blk", "grp"), None),
            P("grp", None),
        ),
        check_vma=False,
    )
```

```python
import functools
import math

import jax
import jax.numpy as jnp
from jax import lax
from jax.experimental import pallas as pl
from jax.experimental.pallas import tpu as pltpu
from jax.sharding import PartitionSpec as P

stability_floor = 1e-06


def as_sent(x):

    def short(part):
        return part.astype(jnp.bfloat16) if part.dtype == jnp.float32 else part

    return jax.tree.map(short, x)


def passed_along(x, axis, by):
    peers = lax.axis_size(axis)
    return lax.ppermute(x, axis, [(i, (i + by) % peers) for i in range(peers)])


def unit_rows(raw):
    row_scale = lax.rsqrt(jnp.sum(raw * raw, axis=1, keepdims=True) + stability_floor)
    return (raw * row_scale, row_scale)


def back_through_norm(normed, row_scale, row_grad):
    along_unit = jnp.sum(normed * row_grad, axis=1, keepdims=True)
    return (row_grad - normed * along_unit) * row_scale


def weighted_sum(query_half, key_half, labels, sigmoid_multiplier, bias_value):
    inner_dots = lax.dot_general(
        query_half, key_half, (((1,), (1,)), ((), ())), preferred_element_type=jnp.float32
    )
    logits = sigmoid_multiplier * inner_dots + bias_value
    pair_weights = (sigmoid_multiplier * (jax.nn.sigmoid(logits) - labels)).astype(jnp.bfloat16)
    return jnp.dot(pair_weights, key_half, preferred_element_type=jnp.float32)


def pass_on(held_rows, direction):
    return jax.tree.map(
        lambda part, own: part.astype(own.dtype),
        passed_along(as_sent(held_rows), "blk", direction),
        held_rows,
    )


def plain_device(
    picture_vectors_prenorm,
    caption_vectors_prenorm,
    matched_caption_ids,
    sharpness_coefficient,
    additive_offset_term,
    heads_mixed_concluding,
    dense_result_adjoint,
    dense_mapping_matrix,
):
    image_units, image_scale = unit_rows(picture_vectors_prenorm)
    text_units, text_scale = unit_rows(caption_vectors_prenorm)
    image_half = image_units.astype(jnp.bfloat16)
    text_half = text_units.astype(jnp.bfloat16)
    sigmoid_multiplier = sharpness_coefficient[0]
    bias_value = additive_offset_term[0]
    own_rows = image_half.shape[0]
    own_first = (lax.axis_index("blk") * lax.axis_size("grp") + lax.axis_index("grp")) * own_rows
    text_index = own_first + lax.broadcasted_iota(jnp.int32, (own_rows, 1), 0)
    grads = (jnp.zeros(image_units.shape, jnp.float32), jnp.zeros(text_units.shape, jnp.float32))
    image_block, text_block, owner_ids = (
        lax.all_gather(image_half, "grp", axis=0, tiled=True),
        lax.all_gather(text_half, "grp", axis=0, tiled=True),
        lax.all_gather(matched_caption_ids, "grp", axis=0, tiled=True),
    )
    group_rows = image_block.shape[0]
    cycle_size = lax.axis_size("blk")
    cycle_place = lax.axis_index("blk")
    streams = [(1, 0, (image_block, text_block, owner_ids))]
    for cycle_step in range(cycle_size):
        next_streams = []
        for direction, offset, held_rows in streams:
            anchor = jnp.remainder(cycle_place - direction * cycle_step, cycle_size)
            absorb_text_block = held_rows[1]
            columns = (
                anchor * group_rows
                + offset
                + lax.broadcasted_iota(jnp.int32, (1, absorb_text_block.shape[0]), 1)
            )
            image_labels = (matched_caption_ids[:, None] == columns).astype(jnp.float32)
            text_labels = (text_index == held_rows[2][None, :]).astype(jnp.float32)
            image_part = weighted_sum(
                image_half, absorb_text_block, image_labels, sigmoid_multiplier, bias_value
            )
            text_part = weighted_sum(
                text_half, held_rows[0], text_labels, sigmoid_multiplier, bias_value
            )
            grads = (grads[0] + image_part, grads[1] + text_part)
            if cycle_step + 1 < cycle_size:
                held_rows = pass_on(held_rows, direction)
            next_streams.append((direction, offset, held_rows))
        streams = next_streams
    image_grad = back_through_norm(image_units, image_scale, grads[0])
    text_grad = back_through_norm(text_units, text_scale, grads[1])
    attn_grad = lax.dot_general(
        dense_result_adjoint,
        lax.all_gather(dense_mapping_matrix, "grp", axis=0, tiled=True),
        (((1,), (1,)), ((), ())),
        preferred_element_type=jnp.float32,
    ).astype(jnp.bfloat16)
    weight_share = lax.psum_scatter(
        lax.dot_general(
            heads_mixed_concluding,
            dense_result_adjoint,
            (((0,), (0,)), ((), ())),
            preferred_element_type=jnp.float32,
        ),
        "grp",
        scatter_dimension=0,
        tiled=True,
    )
    weight_total = lax.psum(weight_share, "blk")
    token_count = heads_mixed_concluding.shape[0] * lax.axis_size("blk") * lax.axis_size("grp")
    weight_grad = weight_total * (1.0 / math.sqrt(token_count))
    return (image_grad, text_grad, attn_grad, weight_grad)


MESH = pl.DeviceIdType.MESH
f32 = jnp.float32
bf16 = jnp.bfloat16


def fused_kernel(
    blks,
    zs,
    scale,
    sharp_ref,
    bias_ref,
    ids_ref,
    pic_hbm,
    cap_hbm,
    heads_hbm,
    adj_hbm,
    w_hbm,
    pic_out,
    cap_out,
    attn_out,
    wgrad_out,
    pic_ref,
    cap_ref,
    heads_ref,
    adj_ref,
    heads_t,
    heads_peer,
    adj_peer,
    w_full,
    part,
    first_in,
    second,
    second_in,
    zsum,
    zsum_in,
    done,
    img,
    img_ids,
    txt,
    img_part,
    img_core_in,
    img_z,
    img_z_in,
    txt_part,
    txt_in,
    load_sem,
    core_sem,
    turn_sem,
    wz_sem,
    ws_sem,
    w1_sem,
    w2_sem,
    wc_sem,
    first_sem,
    second_sem,
    zsum_sem,
    done_sem,
    iz_sem,
    tb_sem,
    ir_sem,
    tr_sem,
):
    b = lax.axis_index("blk")
    g = lax.axis_index("grp")
    z = g // 2
    c = g % 2
    rows, cols = w_hbm.shape
    chunk = rows // blks
    wide = 2 * rows
    own, width = pic_ref.shape
    flip = {1: b + 1 - 2 * lax.rem(b, 2), 2: lax.rem(b + 2, 4)}
    flip[3] = flip[1] + flip[2] - b

    def blk_peer(d):
        return (lax.rem(b + d, blks), g)

    def z_of(d):
        return lax.rem(z + zs + d, zs)

    def z_peer(d):
        return (b, z_of(d) * 2 + c)

    def rows_of(i):
        return pl.ds(pl.multiple_of(i * chunk, 16), chunk)

    partner = (b, z * 2 + 1 - c)
    mine = rows_of(b)

    def rcopy(src, dst, sems, to):
        return pltpu.make_async_remote_copy(
            src_ref=src, dst_ref=dst, send_sem=sems.at[0], recv_sem=sems.at[1],
            device_id=to, device_id_type=MESH,
        )

    sent = []

    def go(src, dst, sems, to):
        copy = rcopy(src, dst, sems, to)
        copy.start()
        sent.append(copy)

    def arrived(dst, sems):
        rcopy(dst, dst, sems, partner).wait_recv()

    barrier = pltpu.get_barrier_semaphore()
    peers = [blk_peer(d) for d in range(1, blks)] + [z_peer(d) for d in range(1, zs)] + [partner]
    for peer in peers:
        pl.semaphore_signal(barrier, inc=1, device_id=peer, device_id_type=MESH)
    loads = [
        pltpu.make_async_copy(src, dst, load_sem.at[i])
        for i, (src, dst) in enumerate(
            [
                (pic_hbm, pic_ref),
                (cap_hbm, cap_ref),
                (heads_hbm, heads_ref),
                (adj_hbm, adj_ref),
                (w_hbm, w_full.at[z, c]),
            ]
        )
    ]
    for load in loads:
        load.start()
    place = lax.broadcasted_iota(jnp.int32, (own, 128), 0)
    tile_ids = jnp.zeros((own, 128), jnp.int32)
    for i in range(own):
        tile_ids = jnp.where(place == i, ids_ref[i], tile_ids)
    img_ids[c, z] = tile_ids
    loads[0].wait()
    loads[1].wait()
    image_units, image_scale = unit_rows(pic_ref[...])
    text_units, text_scale = unit_rows(cap_ref[...])
    img[c, z] = image_units.astype(bf16)
    txt[b] = text_units.astype(bf16)

    pl.semaphore_wait(barrier, len(peers))
    go(adj_hbm, adj_peer, core_sem.at[0], partner)
    for d in range(1, zs):
        go(img.at[c, z], img.at[c, z], iz_sem.at[d - 1, 0], z_peer(d))
        go(img_ids.at[c, z], img_ids.at[c, z], iz_sem.at[d - 1, 1], z_peer(d))
    for d in range(1, blks):
        go(txt.at[b], txt.at[b], tb_sem.at[d - 1], blk_peer(d))
    z_cols = 128 * (cols // 768)
    z_cols += (cols - z_cols) % 256
    span = (cols - z_cols) // 2
    rest = pl.ds(z_cols, 2 * span)
    straight = pl.ds(0, z_cols)
    for d in range(1, zs):
        go(w_hbm.at[mine, rest], w_full.at[z, c, mine, rest], wz_sem.at[d - 1], z_peer(d))
    for d in range(1, zs):
        go(
            w_hbm.at[:, straight], w_full.at[z, c, :, straight], ws_sem.at[d - 1], z_peer(d)
        )

    loads[2].wait()
    for k in range(zs):
        t = z_of(k + 1)
        turned = heads_ref[:, pl.ds(pl.multiple_of(t * wide, 128), wide)].T
        heads_t[0, k] = turned[:rows]
        heads_t[1, k] = turned[rows:]
        go(heads_t.at[1 - c, k], heads_peer.at[k], turn_sem.at[k], partner)

    loads[3].wait()
    arrived(adj_peer, core_sem.at[0])
    half = cols // 2
    for h in range(2):
        for k in range(zs):
            if h == 0:
                arrived(heads_peer.at[k], turn_sem.at[k])
            for j in range(0, half, 256):
                at = h * half + j
                part[h, k, :, j:j + 256] = (
                    jnp.dot(heads_t[c, k], adj_ref[:, at:at + 256], preferred_element_type=f32)
                    + jnp.dot(heads_peer[k], adj_peer[:, at:at + 256], preferred_element_type=f32)
                ).astype(bf16)
            f = 1 + (h + k) % 2
            to = (flip[f], g)
            go(part.at[h, k, rows_of(flip[3])], first_in.at[h, k, 1], first_sem.at[h, k, 1], to)
            go(part.at[h, k, rows_of(flip[f])], first_in.at[h, k, 0], first_sem.at[h, k, 0], to)
    go(w_hbm, w_full.at[z, c], wc_sem.at[0], partner)

    for d in range(1, zs):
        arrived(img.at[c, z_of(-d)], iz_sem.at[d - 1, 0])
        arrived(img_ids.at[c, z_of(-d)], iz_sem.at[d - 1, 1])
    go(img.at[c], img.at[c], core_sem.at[2], partner)
    go(img_ids.at[c], img_ids.at[c], core_sem.at[3], partner)

    def w_piece(e, i, h):
        return w_full.at[z_of(-e), c, rows_of(i), pl.ds(z_cols + h * span, span)]

    def w_first(e):
        arrived(w_full.at[z_of(-e), c, mine, rest], wz_sem.at[e - 1])
        for h in range(2):
            piece = w_piece(e, b, h)
            go(piece, piece, w1_sem.at[e - 1, h], (flip[1 + h], g))

    def w_second(e):
        for h in range(2):
            got = w_piece(e, flip[1 + h], h)
            arrived(got, w1_sem.at[e - 1, h])
            to = (flip[2 - h], g)
            go(got, got, w2_sem.at[e - 1, h, 0], to)
            piece = w_piece(e, b, h)
            go(piece, piece, w2_sem.at[e - 1, h, 1], to)

    def w_core(e):
        arrived(w_full.at[z_of(-e), c, :, straight], ws_sem.at[e - 1])
        for h in range(2):
            arrived(w_piece(e, flip[3], h), w2_sem.at[e - 1, h, 0])
            arrived(w_piece(e, flip[2 - h], h), w2_sem.at[e - 1, h, 1])
        block = w_full.at[z_of(-e), c]
        go(block, block, wc_sem.at[e], partner)

    def own_attn(e):
        zf = z_of(-e)
        arrived(w_full.at[zf, 1 - c], wc_sem.at[e])
        both = w_full[zf].reshape(wide, cols)
        attn_out[:, pl.ds(pl.multiple_of(zf * wide, 128), wide)] = lax.dot_general(
            adj_ref[...], both, (((1,), (1,)), ((), ())), preferred_element_type=f32
        ).astype(bf16)

    def step_two(h, k):
        s = 2 - (h + k) % 2
        arrived(first_in.at[h, k, 1], first_sem.at[h, k, 1])
        second[h, k] = (
            part[h, k, rows_of(flip[s])].astype(f32) + first_in[h, k, 1].astype(f32)
        ).astype(bf16)
        go(second.at[h, k], second_in.at[h, k], second_sem.at[h, k], (flip[s], g))

    def step_three(h, k):
        arrived(first_in.at[h, k, 0], first_sem.at[h, k, 0])
        arrived(second_in.at[h, k], second_sem.at[h, k])
        total = (
            part[h, k, mine].astype(f32)
            + first_in[h, k, 0].astype(f32)
            + second_in[h, k].astype(f32)
        )
        if k < zs - 1:
            zsum[h, k] = total.astype(bf16)
            go(zsum.at[h, k], zsum_in.at[h, k], zsum_sem.at[h, k], z_peer(k + 1))
        return total

    def finish(h, total):
        for k in range(zs - 1):
            arrived(zsum_in.at[h, k], zsum_sem.at[h, k])
            total += zsum_in[h, k].astype(f32)
        done[h, 0] = (total * scale).astype(bf16)
        for d in range(1, blks):
            go(done.at[h, 0], done.at[h, d], done_sem.at[h, d - 1], blk_peer(d))

    w_first(1)
    for k in range(zs):
        step_two(0, k)
    for e in range(2, zs):
        w_first(e)
    for k in range(zs):
        step_two(1, k)

    for d in range(1, blks):
        arrived(txt.at[lax.rem(b + blks - d, blks)], tb_sem.at[d - 1])
    arrived(img.at[1 - c], core_sem.at[2])
    arrived(img_ids.at[1 - c], core_sem.at[3])
    image_rows = 2 * zs * own
    text_rows = blks * own
    images = img[...].reshape(image_rows, width)
    texts = txt[...].reshape(text_rows, width)
    owners = img_ids[...].reshape(image_rows, 128)[:, :1]
    lane = lax.broadcasted_iota(jnp.int32, (image_rows, text_rows), 1)
    column = ((lane // own) * (2 * zs) + g) * own + lane % own
    labels = (owners == column).astype(f32)
    inner_dots = lax.dot_general(
        images, texts, (((1,), (1,)), ((), ())), preferred_element_type=f32
    )
    sharp = sharp_ref[0]
    pair = sharp * (jax.nn.sigmoid(sharp * inner_dots + bias_ref[0]) - labels)
    img_part[...] = jnp.dot(pair.astype(bf16), texts, preferred_element_type=f32).reshape(
        2, zs, own, width
    )
    txt_part[...] = jnp.dot(
        pair.T.astype(bf16), images, preferred_element_type=f32
    ).reshape(blks, own, width)
    go(img_part.at[1 - c], img_core_in, core_sem.at[4], partner)
    for d in range(1, blks):
        to = blk_peer(d)
        go(txt_part.at[to[0]], txt_in.at[d - 1], tr_sem.at[d - 1], to)

    for k in range(zs):
        total_a = step_three(0, k)
        if k == 1:
            w_second(1)
    arrived(img_core_in, core_sem.at[4])
    img_z[...] = img_part[c] + img_core_in[...]
    for d in range(1, zs):
        go(img_z.at[z_of(d)], img_z_in.at[d - 1], ir_sem.at[d - 1], z_peer(d))
    for k in range(zs):
        total_b = step_three(1, k)
        if 1 < k:
            w_second(k)
    loads[4].wait()
    own_attn(0)

    finish(0, total_a)
    w_core(1)
    finish(1, total_b)
    for e in range(2, zs):
        w_core(e)
        own_attn(e - 1)

    image_grad = img_z[z]
    for d in range(1, zs):
        arrived(img_z_in.at[d - 1], ir_sem.at[d - 1])
        image_grad += img_z_in[d - 1]
    pic_out[...] = back_through_norm(image_units, image_scale, image_grad)
    text_grad = txt_part[b]
    for d in range(1, blks):
        arrived(txt_in.at[d - 1], tr_sem.at[d - 1])
        text_grad += txt_in[d - 1]
    cap_out[...] = back_through_norm(text_units, text_scale, text_grad)

    own_attn(zs - 1)
    for h in range(2):
        side = slice(h * half, (h + 1) * half)
        wgrad_out[mine, side] = done[h, 0].astype(f32)
        for d in range(1, blks):
            arrived(done.at[h, d], done_sem.at[h, d - 1])
            wgrad_out[rows_of(lax.rem(b + blks - d, blks)), side] = done[h, d].astype(f32)

    for copy in sent:
        copy.wait_send()


def store_kernel(*refs):
    ins, outs, held, sems = refs[:4], refs[4:8], refs[8:12], refs[12]
    loads = [pltpu.make_async_copy(ins[i], held[i], sems.at[0, i]) for i in range(4)]
    stores = [pltpu.make_async_copy(held[i], outs[i], sems.at[1, i]) for i in range(4)]
    for load in loads:
        load.start()
    for load, store in zip(loads, stores):
        load.wait()
        store.start()
    for store in stores:
        store.wait()


def fused_device(blks, grps, pic, cap, ids, sharp, bias, heads, adj, w):
    zs = grps // 2
    own, width = pic.shape
    tokens, cols = adj.shape
    rows = w.shape[0]
    chunk = rows // blks
    half = cols // 2
    scale = 1.0 / math.sqrt(tokens * blks * grps)
    vmem = pl.BlockSpec(memory_space=pltpu.VMEM)
    smem = pl.BlockSpec(memory_space=pltpu.SMEM)
    hbm = pl.BlockSpec(memory_space=pltpu.HBM)
    dma = pltpu.SemaphoreType.DMA
    grads = pl.pallas_call(
        functools.partial(fused_kernel, blks, zs, scale),
        out_shape=(
            jax.ShapeDtypeStruct(pic.shape, f32),
            jax.ShapeDtypeStruct(cap.shape, f32),
            jax.ShapeDtypeStruct(heads.shape, bf16),
            jax.ShapeDtypeStruct(w.shape, f32),
        ),
        in_specs=[smem] * 3 + [hbm] * 5,
        out_specs=(vmem,) * 4,
        scratch_shapes=[
            pltpu.VMEM(pic.shape, f32),
            pltpu.VMEM(cap.shape, f32),
            pltpu.VMEM((tokens, cols), bf16),
            pltpu.VMEM((tokens, cols), bf16),
            pltpu.VMEM((2, zs, rows, tokens), bf16),
            pltpu.VMEM((zs, rows, tokens), bf16),
            pltpu.VMEM((tokens, cols), bf16),
            pltpu.VMEM((zs, 2, rows, cols), bf16),
            pltpu.VMEM((2, zs, rows, half), bf16),
            pltpu.VMEM((2, zs, 2, chunk, half), bf16),
            pltpu.VMEM((2, zs, chunk, half), bf16),
            pltpu.VMEM((2, zs, chunk, half), bf16),
            pltpu.VMEM((2, zs - 1, chunk, half), bf16),
            pltpu.VMEM((2, zs - 1, chunk, half), bf16),
            pltpu.VMEM((2, blks, chunk, half), bf16),
            pltpu.VMEM((2, zs, own, width), bf16),
            pltpu.VMEM((2, zs, own, 128), jnp.int32),
            pltpu.VMEM((blks, own, width), bf16),
            pltpu.VMEM((2, zs, own, width), f32),
            pltpu.VMEM((zs, own, width), f32),
            pltpu.VMEM((zs, own, width), f32),
            pltpu.VMEM((zs - 1, own, width), f32),
            pltpu.VMEM((blks, own, width), f32),
            pltpu.VMEM((blks - 1, own, width), f32),
            dma((5,)),
            dma((5, 2)),
            dma((zs, 2)),
            dma((zs - 1, 2)),
            dma((zs - 1, 2)),
            dma((zs - 1, 2, 2)),
            dma((zs - 1, 2, 2, 2)),
            dma((zs, 2)),
            dma((2, zs, 2, 2)),
            dma((2, zs, 2)),
            dma((2, zs - 1, 2)),
            dma((2, blks - 1, 2)),
            dma((zs - 1, 2, 2)),
            dma((blks - 1, 2)),
            dma((zs - 1, 2)),
            dma((blks - 1, 2)),
        ],
        compiler_params=pltpu.CompilerParams(
            collective_id=0, has_side_effects=True, vmem_limit_bytes=56 * 1024 * 1024
        ),
        cost_estimate=pl.CostEstimate(
            flops=4 * tokens * cols * cols, bytes_accessed=8 * tokens * cols, transcendentals=0
        ),
    )(sharp, bias, ids, pic, cap, heads, adj, w)
    return pl.pallas_call(
        store_kernel,
        out_shape=tuple(jax.ShapeDtypeStruct(x.shape, x.dtype) for x in grads),
        in_specs=[hbm] * 4,
        out_specs=(hbm,) * 4,
        scratch_shapes=[pltpu.VMEM(x.shape, x.dtype) for x in grads] + [dma((2, 4))],
        compiler_params=pltpu.CompilerParams(vmem_limit_bytes=56 * 1024 * 1024),
    )(*grads)


def per_device(pic, cap, ids, sharp, bias, heads, adj, w):
    blks = lax.axis_size("blk")
    grps = lax.axis_size("grp")
    own = pic.shape[0]
    rows, cols = w.shape
    fits = (
        grps % 2 == 0
        and grps >= 4
        and blks == 4
        and rows % (16 * blks) == 0
        and (2 * rows) % 128 == 0
        and heads.shape[1] == rows * grps
        and cols == heads.shape[1]
        and own % 16 == 0
        and cols % 512 == 0
    )
    if not fits:
        return plain_device(pic, cap, ids, sharp, bias, heads, adj, w)
    return fused_device(blks, grps, pic, cap, ids, sharp, bias, heads, adj, w)


def solution(mesh):
    placed = (
        P(("blk", "grp"), None),
        P(("blk", "grp"), None),
        P(("blk", "grp")),
        P(),
        P(),
        P(("blk", "grp"), None),
        P(("blk", "grp"), None),
        P("grp", None),
    )
    return jax.shard_map(
        per_device,
        mesh=mesh,
        in_specs=placed,
        out_specs=(
            P(("blk", "grp"), None),
            P(("blk", "grp"), None),
            P(("blk", "grp"), None),
            P("grp", None),
        ),
        check_vma=False,
    )
```

```python
import functools
import math

import jax
import jax.numpy as jnp
from jax import lax
from jax.experimental import pallas as pl
from jax.experimental.pallas import tpu as pltpu
from jax.sharding import PartitionSpec as P

stability_floor = 1e-06


def as_sent(x):

    def short(part):
        return part.astype(jnp.bfloat16) if part.dtype == jnp.float32 else part

    return jax.tree.map(short, x)


def passed_along(x, axis, by):
    peers = lax.axis_size(axis)
    return lax.ppermute(x, axis, [(i, (i + by) % peers) for i in range(peers)])


def unit_rows(raw):
    row_scale = lax.rsqrt(jnp.sum(raw * raw, axis=1, keepdims=True) + stability_floor)
    return (raw * row_scale, row_scale)


def back_through_norm(normed, row_scale, row_grad):
    along_unit = jnp.sum(normed * row_grad, axis=1, keepdims=True)
    return (row_grad - normed * along_unit) * row_scale


def weighted_sum(query_half, key_half, labels, sigmoid_multiplier, bias_value):
    inner_dots = lax.dot_general(
        query_half, key_half, (((1,), (1,)), ((), ())), preferred_element_type=jnp.float32
    )
    logits = sigmoid_multiplier * inner_dots + bias_value
    pair_weights = (sigmoid_multiplier * (jax.nn.sigmoid(logits) - labels)).astype(jnp.bfloat16)
    return jnp.dot(pair_weights, key_half, preferred_element_type=jnp.float32)


def pass_on(held_rows, direction):
    return jax.tree.map(
        lambda part, own: part.astype(own.dtype),
        passed_along(as_sent(held_rows), "blk", direction),
        held_rows,
    )


def plain_device(
    picture_vectors_prenorm,
    caption_vectors_prenorm,
    matched_caption_ids,
    sharpness_coefficient,
    additive_offset_term,
    heads_mixed_concluding,
    dense_result_adjoint,
    dense_mapping_matrix,
):
    image_units, image_scale = unit_rows(picture_vectors_prenorm)
    text_units, text_scale = unit_rows(caption_vectors_prenorm)
    image_half = image_units.astype(jnp.bfloat16)
    text_half = text_units.astype(jnp.bfloat16)
    sigmoid_multiplier = sharpness_coefficient[0]
    bias_value = additive_offset_term[0]
    own_rows = image_half.shape[0]
    own_first = (lax.axis_index("blk") * lax.axis_size("grp") + lax.axis_index("grp")) * own_rows
    text_index = own_first + lax.broadcasted_iota(jnp.int32, (own_rows, 1), 0)
    grads = (jnp.zeros(image_units.shape, jnp.float32), jnp.zeros(text_units.shape, jnp.float32))
    image_block, text_block, owner_ids = (
        lax.all_gather(image_half, "grp", axis=0, tiled=True),
        lax.all_gather(text_half, "grp", axis=0, tiled=True),
        lax.all_gather(matched_caption_ids, "grp", axis=0, tiled=True),
    )
    group_rows = image_block.shape[0]
    cycle_size = lax.axis_size("blk")
    cycle_place = lax.axis_index("blk")
    streams = [(1, 0, (image_block, text_block, owner_ids))]
    for cycle_step in range(cycle_size):
        next_streams = []
        for direction, offset, held_rows in streams:
            anchor = jnp.remainder(cycle_place - direction * cycle_step, cycle_size)
            absorb_text_block = held_rows[1]
            columns = (
                anchor * group_rows
                + offset
                + lax.broadcasted_iota(jnp.int32, (1, absorb_text_block.shape[0]), 1)
            )
            image_labels = (matched_caption_ids[:, None] == columns).astype(jnp.float32)
            text_labels = (text_index == held_rows[2][None, :]).astype(jnp.float32)
            image_part = weighted_sum(
                image_half, absorb_text_block, image_labels, sigmoid_multiplier, bias_value
            )
            text_part = weighted_sum(
                text_half, held_rows[0], text_labels, sigmoid_multiplier, bias_value
            )
            grads = (grads[0] + image_part, grads[1] + text_part)
            if cycle_step + 1 < cycle_size:
                held_rows = pass_on(held_rows, direction)
            next_streams.append((direction, offset, held_rows))
        streams = next_streams
    image_grad = back_through_norm(image_units, image_scale, grads[0])
    text_grad = back_through_norm(text_units, text_scale, grads[1])
    attn_grad = lax.dot_general(
        dense_result_adjoint,
        lax.all_gather(dense_mapping_matrix, "grp", axis=0, tiled=True),
        (((1,), (1,)), ((), ())),
        preferred_element_type=jnp.float32,
    ).astype(jnp.bfloat16)
    weight_share = lax.psum_scatter(
        lax.dot_general(
            heads_mixed_concluding,
            dense_result_adjoint,
            (((0,), (0,)), ((), ())),
            preferred_element_type=jnp.float32,
        ),
        "grp",
        scatter_dimension=0,
        tiled=True,
    )
    weight_total = lax.psum(weight_share, "blk")
    token_count = heads_mixed_concluding.shape[0] * lax.axis_size("blk") * lax.axis_size("grp")
    weight_grad = weight_total * (1.0 / math.sqrt(token_count))
    return (image_grad, text_grad, attn_grad, weight_grad)


MESH = pl.DeviceIdType.MESH
f32 = jnp.float32
bf16 = jnp.bfloat16


def fused_kernel(
    blks,
    zs,
    scale,
    sharp_ref,
    bias_ref,
    ids_ref,
    pic_hbm,
    cap_hbm,
    heads_hbm,
    adj_hbm,
    w_hbm,
    pic_out,
    cap_out,
    attn_hbm,
    wgrad_hbm,
    attn_out,
    wgrad_out,
    pic_ref,
    cap_ref,
    heads_ref,
    adj_ref,
    heads_t,
    heads_peer,
    adj_peer,
    w_full,
    part,
    first_in,
    second,
    second_in,
    zsum,
    zsum_in,
    done,
    img,
    img_ids,
    txt,
    img_part,
    img_core_in,
    img_z,
    img_z_in,
    txt_part,
    txt_in,
    load_sem,
    core_sem,
    turn_sem,
    wz_sem,
    ws_sem,
    w1_sem,
    w2_sem,
    wc_sem,
    first_sem,
    second_sem,
    zsum_sem,
    done_sem,
    iz_sem,
    tb_sem,
    ir_sem,
    tr_sem,
    attn_sem,
    wgrad_sem,
):
    b = lax.axis_index("blk")
    g = lax.axis_index("grp")
    z = g // 2
    c = g % 2
    rows, cols = w_hbm.shape
    chunk = rows // blks
    wide = 2 * rows
    own, width = pic_ref.shape
    flip = {1: b + 1 - 2 * lax.rem(b, 2), 2: lax.rem(b + 2, 4)}
    flip[3] = flip[1] + flip[2] - b

    def blk_peer(d):
        return (lax.rem(b + d, blks), g)

    def z_of(d):
        return lax.rem(z + zs + d, zs)

    def z_peer(d):
        return (b, z_of(d) * 2 + c)

    def rows_of(i):
        return pl.ds(pl.multiple_of(i * chunk, 16), chunk)

    partner = (b, z * 2 + 1 - c)
    mine = rows_of(b)

    def rcopy(src, dst, sems, to):
        return pltpu.make_async_remote_copy(
            src_ref=src, dst_ref=dst, send_sem=sems.at[0], recv_sem=sems.at[1],
            device_id=to, device_id_type=MESH,
        )

    sent = []

    def go(src, dst, sems, to):
        copy = rcopy(src, dst, sems, to)
        copy.start()
        sent.append(copy)

    def arrived(dst, sems):
        rcopy(dst, dst, sems, partner).wait_recv()

    barrier = pltpu.get_barrier_semaphore()
    peers = [blk_peer(d) for d in range(1, blks)] + [z_peer(d) for d in range(1, zs)] + [partner]
    for peer in peers:
        pl.semaphore_signal(barrier, inc=1, device_id=peer, device_id_type=MESH)
    loads = [
        pltpu.make_async_copy(src, dst, load_sem.at[i])
        for i, (src, dst) in enumerate(
            [
                (pic_hbm, pic_ref),
                (cap_hbm, cap_ref),
                (heads_hbm, heads_ref),
                (adj_hbm, adj_ref),
                (w_hbm, w_full.at[z, c]),
            ]
        )
    ]
    for load in loads:
        load.start()
    place = lax.broadcasted_iota(jnp.int32, (own, 128), 0)
    tile_ids = jnp.zeros((own, 128), jnp.int32)
    for i in range(own):
        tile_ids = jnp.where(place == i, ids_ref[i], tile_ids)
    img_ids[c, z] = tile_ids
    loads[0].wait()
    loads[1].wait()
    image_units, image_scale = unit_rows(pic_ref[...])
    text_units, text_scale = unit_rows(cap_ref[...])
    img[c, z] = image_units.astype(bf16)
    txt[b] = text_units.astype(bf16)

    pl.semaphore_wait(barrier, len(peers))
    go(adj_hbm, adj_peer, core_sem.at[0], partner)
    for d in range(1, zs):
        go(img.at[c, z], img.at[c, z], iz_sem.at[d - 1, 0], z_peer(d))
        go(img_ids.at[c, z], img_ids.at[c, z], iz_sem.at[d - 1, 1], z_peer(d))
    for d in range(1, blks):
        go(txt.at[b], txt.at[b], tb_sem.at[d - 1], blk_peer(d))
    z_cols = 128 * (cols // 768)
    z_cols += (cols - z_cols) % 256
    span = (cols - z_cols) // 2
    rest = pl.ds(z_cols, 2 * span)
    straight = pl.ds(0, z_cols)
    for d in range(1, zs):
        go(w_hbm.at[mine, rest], w_full.at[z, c, mine, rest], wz_sem.at[d - 1], z_peer(d))
    for d in range(1, zs):
        go(
            w_hbm.at[:, straight], w_full.at[z, c, :, straight], ws_sem.at[d - 1], z_peer(d)
        )

    loads[2].wait()
    for k in range(zs):
        t = z_of(k + 1)
        turned = heads_ref[:, pl.ds(pl.multiple_of(t * wide, 128), wide)].T
        heads_t[0, k] = turned[:rows]
        heads_t[1, k] = turned[rows:]
        go(heads_t.at[1 - c, k], heads_peer.at[k], turn_sem.at[k], partner)

    loads[3].wait()
    arrived(adj_peer, core_sem.at[0])
    half = cols // 2
    for h in range(2):
        for k in range(zs):
            if h == 0:
                arrived(heads_peer.at[k], turn_sem.at[k])
            for j in range(0, half, 256):
                at = h * half + j
                part[h, k, :, j:j + 256] = (
                    jnp.dot(heads_t[c, k], adj_ref[:, at:at + 256], preferred_element_type=f32)
                    + jnp.dot(heads_peer[k], adj_peer[:, at:at + 256], preferred_element_type=f32)
                ).astype(bf16)
            f = 1 + (h + k) % 2
            to = (flip[f], g)
            go(part.at[h, k, rows_of(flip[3])], first_in.at[h, k, 1], first_sem.at[h, k, 1], to)
            go(part.at[h, k, rows_of(flip[f])], first_in.at[h, k, 0], first_sem.at[h, k, 0], to)
    go(w_hbm, w_full.at[z, c], wc_sem.at[0], partner)

    for d in range(1, zs):
        arrived(img.at[c, z_of(-d)], iz_sem.at[d - 1, 0])
        arrived(img_ids.at[c, z_of(-d)], iz_sem.at[d - 1, 1])
    go(img.at[c], img.at[c], core_sem.at[2], partner)
    go(img_ids.at[c], img_ids.at[c], core_sem.at[3], partner)

    kept = []

    def keep(src, dst, sem):
        copy = pltpu.make_async_copy(src, dst, sem)
        copy.start()
        kept.append(copy)

    def w_piece(e, i, h):
        return w_full.at[z_of(-e), c, rows_of(i), pl.ds(z_cols + h * span, span)]

    def w_first(e):
        arrived(w_full.at[z_of(-e), c, mine, rest], wz_sem.at[e - 1])
        for h in range(2):
            piece = w_piece(e, b, h)
            go(piece, piece, w1_sem.at[e - 1, h], (flip[1 + h], g))

    def w_second(e):
        for h in range(2):
            got = w_piece(e, flip[1 + h], h)
            arrived(got, w1_sem.at[e - 1, h])
            to = (flip[2 - h], g)
            go(got, got, w2_sem.at[e - 1, h, 0], to)
            piece = w_piece(e, b, h)
            go(piece, piece, w2_sem.at[e - 1, h, 1], to)

    def w_core(e):
        arrived(w_full.at[z_of(-e), c, :, straight], ws_sem.at[e - 1])
        for h in range(2):
            arrived(w_piece(e, flip[3], h), w2_sem.at[e - 1, h, 0])
            arrived(w_piece(e, flip[2 - h], h), w2_sem.at[e - 1, h, 1])
        block = w_full.at[z_of(-e), c]
        go(block, block, wc_sem.at[e], partner)

    def own_attn(e):
        zf = z_of(-e)
        arrived(w_full.at[zf, 1 - c], wc_sem.at[e])
        both = w_full[zf].reshape(wide, cols)
        block = pl.ds(pl.multiple_of(zf * wide, 128), wide)
        attn_out[:, block] = lax.dot_general(
            adj_ref[...], both, (((1,), (1,)), ((), ())), preferred_element_type=f32
        ).astype(bf16)
        keep(attn_out.at[:, block], attn_hbm.at[:, block], attn_sem.at[e])

    def step_two(h, k):
        s = 2 - (h + k) % 2
        arrived(first_in.at[h, k, 1], first_sem.at[h, k, 1])
        second[h, k] = (
            part[h, k, rows_of(flip[s])].astype(f32) + first_in[h, k, 1].astype(f32)
        ).astype(bf16)
        go(second.at[h, k], second_in.at[h, k], second_sem.at[h, k], (flip[s], g))

    def step_three(h, k):
        arrived(first_in.at[h, k, 0], first_sem.at[h, k, 0])
        arrived(second_in.at[h, k], second_sem.at[h, k])
        total = (
            part[h, k, mine].astype(f32)
            + first_in[h, k, 0].astype(f32)
            + second_in[h, k].astype(f32)
        )
        if k < zs - 1:
            zsum[h, k] = total.astype(bf16)
            go(zsum.at[h, k], zsum_in.at[h, k], zsum_sem.at[h, k], z_peer(k + 1))
        return total

    def finish(h, total):
        for k in range(zs - 1):
            arrived(zsum_in.at[h, k], zsum_sem.at[h, k])
            total += zsum_in[h, k].astype(f32)
        done[h, 0] = (total * scale).astype(bf16)
        for d in range(1, blks):
            go(done.at[h, 0], done.at[h, d], done_sem.at[h, d - 1], blk_peer(d))

    w_first(1)
    for k in range(zs):
        step_two(0, k)
    for e in range(2, zs):
        w_first(e)
    for k in range(zs):
        step_two(1, k)

    for d in range(1, blks):
        arrived(txt.at[lax.rem(b + blks - d, blks)], tb_sem.at[d - 1])
    arrived(img.at[1 - c], core_sem.at[2])
    arrived(img_ids.at[1 - c], core_sem.at[3])
    image_rows = 2 * zs * own
    text_rows = blks * own
    images = img[...].reshape(image_rows, width)
    texts = txt[...].reshape(text_rows, width)
    owners = img_ids[...].reshape(image_rows, 128)[:, :1]
    lane = lax.broadcasted_iota(jnp.int32, (image_rows, text_rows), 1)
    column = ((lane // own) * (2 * zs) + g) * own + lane % own
    labels = (owners == column).astype(f32)
    inner_dots = lax.dot_general(
        images, texts, (((1,), (1,)), ((), ())), preferred_element_type=f32
    )
    sharp = sharp_ref[0]
    pair = sharp * (jax.nn.sigmoid(sharp * inner_dots + bias_ref[0]) - labels)
    img_part[...] = jnp.dot(pair.astype(bf16), texts, preferred_element_type=f32).reshape(
        2, zs, own, width
    )
    txt_part[...] = jnp.dot(
        pair.T.astype(bf16), images, preferred_element_type=f32
    ).reshape(blks, own, width)
    go(img_part.at[1 - c], img_core_in, core_sem.at[4], partner)
    for d in range(1, blks):
        to = blk_peer(d)
        go(txt_part.at[to[0]], txt_in.at[d - 1], tr_sem.at[d - 1], to)

    for k in range(zs):
        total_a = step_three(0, k)
        if k == 1:
            w_second(1)
    arrived(img_core_in, core_sem.at[4])
    img_z[...] = img_part[c] + img_core_in[...]
    for d in range(1, zs):
        go(img_z.at[z_of(d)], img_z_in.at[d - 1], ir_sem.at[d - 1], z_peer(d))
    for k in range(zs):
        total_b = step_three(1, k)
        if 1 < k:
            w_second(k)
    loads[4].wait()
    own_attn(0)

    finish(0, total_a)
    w_core(1)
    finish(1, total_b)
    for e in range(2, zs):
        w_core(e)
        own_attn(e - 1)

    image_grad = img_z[z]
    for d in range(1, zs):
        arrived(img_z_in.at[d - 1], ir_sem.at[d - 1])
        image_grad += img_z_in[d - 1]
    pic_out[...] = back_through_norm(image_units, image_scale, image_grad)
    text_grad = txt_part[b]
    for d in range(1, blks):
        arrived(txt_in.at[d - 1], tr_sem.at[d - 1])
        text_grad += txt_in[d - 1]
    cap_out[...] = back_through_norm(text_units, text_scale, text_grad)

    own_attn(zs - 1)
    for h in range(2):
        side = slice(h * half, (h + 1) * half)
        for d in range(blks):
            if d > 0:
                arrived(done.at[h, d], done_sem.at[h, d - 1])
            there = rows_of(lax.rem(b + blks - d, blks))
            wgrad_out[there, side] = done[h, d].astype(f32)
            keep(wgrad_out.at[there, side], wgrad_hbm.at[there, side], wgrad_sem.at[h, d])

    for copy in sent:
        copy.wait_send()
    for copy in kept:
        copy.wait()


def store_kernel(*refs):
    ins, outs, held, sems = refs[:4], refs[4:8], refs[8:12], refs[12]
    pieces = []
    for i in (2, 3, 0, 1):
        size = ins[i].shape[0]
        step = size // 4 if size % 64 == 0 else size
        pieces += [(i, pl.ds(at, step)) for at in range(0, size, step)]
    loads, stores = [], []
    for n, (i, at) in enumerate(pieces):
        loads.append(pltpu.make_async_copy(ins[i].at[at], held[i].at[at], sems.at[0, n]))
        stores.append(pltpu.make_async_copy(held[i].at[at], outs[i].at[at], sems.at[1, n]))
    for load in loads:
        load.start()
    for load, store in zip(loads, stores):
        load.wait()
        store.start()
    for store in stores:
        store.wait()


def fused_device(blks, grps, pic, cap, ids, sharp, bias, heads, adj, w):
    zs = grps // 2
    own, width = pic.shape
    tokens, cols = adj.shape
    rows = w.shape[0]
    chunk = rows // blks
    half = cols // 2
    scale = 1.0 / math.sqrt(tokens * blks * grps)
    vmem = pl.BlockSpec(memory_space=pltpu.VMEM)
    smem = pl.BlockSpec(memory_space=pltpu.SMEM)
    hbm = pl.BlockSpec(memory_space=pltpu.HBM)
    dma = pltpu.SemaphoreType.DMA
    grads = pl.pallas_call(
        functools.partial(fused_kernel, blks, zs, scale),
        out_shape=(
            jax.ShapeDtypeStruct(pic.shape, f32),
            jax.ShapeDtypeStruct(cap.shape, f32),
            jax.ShapeDtypeStruct(heads.shape, bf16),
            jax.ShapeDtypeStruct(w.shape, f32),
        ),
        in_specs=[smem] * 3 + [hbm] * 5,
        out_specs=(vmem, vmem, hbm, hbm),
        scratch_shapes=[
            pltpu.VMEM(heads.shape, bf16),
            pltpu.VMEM(w.shape, f32),
            pltpu.VMEM(pic.shape, f32),
            pltpu.VMEM(cap.shape, f32),
            pltpu.VMEM((tokens, cols), bf16),
            pltpu.VMEM((tokens, cols), bf16),
            pltpu.VMEM((2, zs, rows, tokens), bf16),
            pltpu.VMEM((zs, rows, tokens), bf16),
            pltpu.VMEM((tokens, cols), bf16),
            pltpu.VMEM((zs, 2, rows, cols), bf16),
            pltpu.VMEM((2, zs, rows, half), bf16),
            pltpu.VMEM((2, zs, 2, chunk, half), bf16),
            pltpu.VMEM((2, zs, chunk, half), bf16),
            pltpu.VMEM((2, zs, chunk, half), bf16),
            pltpu.VMEM((2, zs - 1, chunk, half), bf16),
            pltpu.VMEM((2, zs - 1, chunk, half), bf16),
            pltpu.VMEM((2, blks, chunk, half), bf16),
            pltpu.VMEM((2, zs, own, width), bf16),
            pltpu.VMEM((2, zs, own, 128), jnp.int32),
            pltpu.VMEM((blks, own, width), bf16),
            pltpu.VMEM((2, zs, own, width), f32),
            pltpu.VMEM((zs, own, width), f32),
            pltpu.VMEM((zs, own, width), f32),
            pltpu.VMEM((zs - 1, own, width), f32),
            pltpu.VMEM((blks, own, width), f32),
            pltpu.VMEM((blks - 1, own, width), f32),
            dma((5,)),
            dma((5, 2)),
            dma((zs, 2)),
            dma((zs - 1, 2)),
            dma((zs - 1, 2)),
            dma((zs - 1, 2, 2)),
            dma((zs - 1, 2, 2, 2)),
            dma((zs, 2)),
            dma((2, zs, 2, 2)),
            dma((2, zs, 2)),
            dma((2, zs - 1, 2)),
            dma((2, blks - 1, 2)),
            dma((zs - 1, 2, 2)),
            dma((blks - 1, 2)),
            dma((zs - 1, 2)),
            dma((blks - 1, 2)),
            dma((zs,)),
            dma((2, blks)),
        ],
        compiler_params=pltpu.CompilerParams(
            collective_id=0, has_side_effects=True, vmem_limit_bytes=56 * 1024 * 1024
        ),
        cost_estimate=pl.CostEstimate(
            flops=4 * tokens * cols * cols, bytes_accessed=8 * tokens * cols, transcendentals=0
        ),
    )(sharp, bias, ids, pic, cap, heads, adj, w)
    return pl.pallas_call(
        store_kernel,
        out_shape=tuple(jax.ShapeDtypeStruct(x.shape, x.dtype) for x in grads),
        in_specs=[hbm] * 4,
        out_specs=(hbm,) * 4,
        scratch_shapes=[pltpu.VMEM(x.shape, x.dtype) for x in grads] + [dma((2, 16))],
        compiler_params=pltpu.CompilerParams(vmem_limit_bytes=56 * 1024 * 1024),
    )(*grads)


def per_device(pic, cap, ids, sharp, bias, heads, adj, w):
    blks = lax.axis_size("blk")
    grps = lax.axis_size("grp")
    own = pic.shape[0]
    rows, cols = w.shape
    fits = (
        grps % 2 == 0
        and grps >= 4
        and blks == 4
        and rows % (16 * blks) == 0
        and (2 * rows) % 128 == 0
        and heads.shape[1] == rows * grps
        and cols == heads.shape[1]
        and own % 16 == 0
        and cols % 512 == 0
    )
    if not fits:
        return plain_device(pic, cap, ids, sharp, bias, heads, adj, w)
    return fused_device(blks, grps, pic, cap, ids, sharp, bias, heads, adj, w)


def solution(mesh):
    placed = (
        P(("blk", "grp"), None),
        P(("blk", "grp"), None),
        P(("blk", "grp")),
        P(),
        P(),
        P(("blk", "grp"), None),
        P(("blk", "grp"), None),
        P("grp", None),
    )
    return jax.shard_map(
        per_device,
        mesh=mesh,
        in_specs=placed,
        out_specs=(
            P(("blk", "grp"), None),
            P(("blk", "grp"), None),
            P(("blk", "grp"), None),
            P("grp", None),
        ),
        check_vma=False,
    )
```
